512 devices in a mesh: dp: 128 (over y, z, core), mp: 4 (over x).
Axes of the slice: x: 4, y: 4, z: 16, core: 2. Of those that a mesh axis runs over, the one named last changes fastest.
Arguments:
- queries: bfloat16 [16384, 2048], P('dp', 'mp'), may hold values from -400 to 400
- encodings: bfloat16 [16384, 896], P('dp'), may hold values from -24 to 24
- kv_weight: bfloat16 [896, 2, 2048], P('dp', None, 'mp'), may hold values from -0.1875 to 0.1875
- pair_list: int32 [256, 2], P('dp'), may hold values from 0 to 127, as said below
- cotangent: bfloat16 [16384, 2048], P('dp', 'mp'), may hold values from -6 to 6
Outputs:
- attended: bfloat16 [16384, 2048], P('dp', 'mp')
- query_grad: bfloat16 [16384, 2048], P('dp', 'mp')
- encoding_grad: bfloat16 [16384, 896], P('dp', 'mp')
- weight_grad: float32 [896, 2, 2048], P('dp', None, 'mp')
The draws below stay inside these ranges and needn't reach their ends.
Inputs may be any that keep to these rules, and one draw needn't show every extreme that they name: Each dp device owns one neighbour block, block n belongs to dp device n, and pair_list[c, j] is at most 2 positions away from c // 2 along dp, counted around the cycle of 128 devices.
All inputs are finite; a program needn't handle non-finite values.
Results may differ from the reference program's by a relative error of at most 0.034.
The reference program's roundings to bfloat16 on the way count: a program that leaves them out, or rounds other values in their place, can miss the bound.
Values may be sent and summed in bfloat16 or wider, within the bound.
No kernel may reach another device: no remote copies, remote signals or barrier semaphores. Data moves between devices by JAX's collectives and lax.ppermute only.
A program may use at most 64 MiB of HBM per device.

```python
import jax
import jax.numpy as jnp
from jax import lax

HEADS = 16
HD = 128
ENC = 896
SPAN = 64
NROWS = 128
NBR = 2
REACH = 2
CH_DEV = 2
SLOTS = 1
SPANS = 256
TOKENS = 16384
NEIGH = 128
N_DP = 128
N_MP = 4


def draw_queries(key, part):
    key = jax.random.fold_in(key, 11)
    first, second = jax.random.split(key)
    base = jax.random.normal(first, (TOKENS, HEADS * HD), jnp.float32)
    scales = jnp.exp(jax.random.uniform(second, (TOKENS, 1), jnp.float32, -0.5, 0.5))
    return jnp.clip(base * scales, -400.0, 400.0).astype(jnp.bfloat16)


def draw_pair_list(key, part):
    key = jax.random.fold_in(key, 23)
    first, second = jax.random.split(key)
    span_device = jnp.arange(SPANS, dtype=jnp.int32)[:, None] // CH_DEV
    offsets = jax.random.randint(first, (SPANS, NBR), -REACH, REACH + 1, dtype=jnp.int32)
    slot_draws = jax.random.randint(second, (SPANS, NBR, 2), 0, SLOTS, dtype=jnp.int32)
    slot_index = jnp.min(slot_draws, axis=-1)
    owners = (span_device + offsets) % N_DP
    block_ids = owners * SLOTS + slot_index
    block_ids = block_ids.at[0, 0].set(N_DP * SLOTS - 1).at[0, 1].set(0)
    return block_ids.astype(jnp.int32)


def spiked(entries, key, source, target, blocks, factor):
    def block_of(axis_at):
        return (jnp.arange(entries.shape[axis_at]) // (entries.shape[axis_at] // blocks)).reshape((-1,) + (1,) * (entries.ndim - 1 - axis_at))

    one_side = jax.random.permutation(key, blocks)[block_of(target)]
    second = (block_of(target) + blocks // 2) % blocks
    return jnp.where((block_of(source) == one_side) | (block_of(source) == second), factor * entries, entries)


def block_scale(key, dims, cuts, smallest, top_value):
    def one(position, blocks):
        heights = jax.random.uniform(jax.random.fold_in(jax.random.fold_in(key, 6), position), (blocks,), jnp.float32, smallest / len(cuts), top_value / len(cuts))
        return jnp.repeat(jnp.exp(heights), dims[position] // blocks).reshape((-1,) + (1,) * (len(dims) - position - 1))

    loudness = one(*cuts[0])
    for cut in cuts[1:]:
        loudness = loudness * one(*cut)
    return loudness


def normal_values(rng, shape, spread, limit, shards=(), kind=jnp.bfloat16):
    entries = spread * jax.random.normal(rng, shape, jnp.float32)
    if shards:
        entries = entries * block_scale(rng, shape, shards, -0.22, 0.18)
    return jnp.clip(entries, -limit, limit).astype(kind)


def noise_with(stream_key, shape, scale, limit, shards, heavy, kind=jnp.bfloat16):
    drawn = scale * jax.random.normal(stream_key, shape, jnp.float32)
    if shards:
        drawn = drawn * block_scale(stream_key, shape, shards, -0.22, 0.18)
    return jnp.clip(spiked(drawn, jax.random.fold_in(stream_key, 3), *heavy), -limit, limit).astype(kind)


def setup_inputs(seed: int = 0) -> dict:
    streams_of = jax.random.split(jax.random.key(seed), 6)
    queries = draw_queries(jax.random.fold_in(streams_of[5], 71), 0)
    encodings = noise_with(streams_of[1], (NEIGH * NROWS, ENC), 1.0, 24.0, ((0, 128),), (0, 1, 128, 5.5))
    kv_weight = normal_values(streams_of[2], (ENC, 2, HEADS * HD), ENC ** -0.5, 0.1875, ((0, 128), (2, 4)))
    pair_list = draw_pair_list(jax.random.fold_in(streams_of[5], 71), 0)
    cotangent = normal_values(streams_of[4], (TOKENS, HEADS * HD), 1.0, 6.0, ((0, 128), (1, 4)))
    return {"queries": queries, "encodings": encodings, "kv_weight": kv_weight, "pair_list": pair_list, "cotangent": cotangent}


def reference(queries, encodings, kv_weight, pair_list, cotangent):
    width = HEADS * HD
    factor = 1.0 / (HD ** 0.5)
    projected = jnp.einsum('re,etx->rtx', encodings.astype(jnp.float32), kv_weight.astype(jnp.float32), precision=lax.Precision.HIGHEST).astype(jnp.bfloat16)
    blocks = projected.reshape(NEIGH, NROWS, 2, HEADS, HD)
    query_groups = queries.reshape(N_DP, CH_DEV, SPAN, HEADS, HD)
    grad_groups = cotangent.reshape(N_DP, CH_DEV, SPAN, HEADS, HD)
    pair_groups = pair_list.reshape(N_DP, CH_DEV * NBR).astype(jnp.int32)

    def group(carry, inputs):
        query_rows, grad_rows, pair_ids = inputs
        chosen = blocks[pair_ids].reshape(CH_DEV, NBR * NROWS, 2, HEADS, HD)
        keys = chosen[:, :, 0].astype(jnp.float32)
        values = chosen[:, :, 1].astype(jnp.float32)
        query_f = query_rows.astype(jnp.float32)
        grad_f = grad_rows.astype(jnp.float32)
        scores = jnp.einsum('cqhd,ckhd->chqk', query_f, keys) * factor
        probs = jax.nn.softmax(scores, axis=-1)
        probs_b = probs.astype(jnp.bfloat16).astype(jnp.float32)
        attended = jnp.einsum('chqk,ckhd->cqhd', probs_b, values).astype(jnp.bfloat16)
        dprobs = jnp.einsum('cqhd,ckhd->chqk', grad_f, values)
        delta = jnp.sum(probs * dprobs, axis=-1, keepdims=True)
        dscores = (probs * (dprobs - delta) * factor).astype(jnp.bfloat16).astype(jnp.float32)
        query_grad = jnp.einsum('chqk,ckhd->cqhd', dscores, keys).astype(jnp.bfloat16)
        key_grad = jnp.einsum('chqk,cqhd->ckhd', dscores, query_f)
        value_grad = jnp.einsum('chqk,cqhd->ckhd', probs_b, grad_f)
        stacked = jnp.stack([key_grad, value_grad], axis=2).reshape(CH_DEV * NBR, NROWS, 2, HEADS, HD)
        carry = carry.at[pair_ids].add(stacked)
        return carry, (attended, query_grad)

    start = jnp.zeros((NEIGH, NROWS, 2, HEADS, HD), jnp.float32)
    block_grad, outputs = lax.scan(group, start, (query_groups, grad_groups, pair_groups))
    attended = outputs[0].reshape(TOKENS, width)
    query_grad = outputs[1].reshape(TOKENS, width)
    block_grad_b = block_grad.astype(jnp.bfloat16).reshape(NEIGH * NROWS, 2, width)
    grad_split = block_grad_b.astype(jnp.float32).reshape(NEIGH * NROWS, 2, N_MP, width // N_MP)
    weight_split = kv_weight.astype(jnp.float32).reshape(ENC, 2, N_MP, width // N_MP)
    partials = jnp.einsum('rtgx,etgx->gre', grad_split, weight_split, precision=lax.Precision.HIGHEST).astype(jnp.bfloat16)
    partials = lax.optimization_barrier(partials)
    encoding_grad = jnp.sum(partials.astype(jnp.float32), axis=0).astype(jnp.bfloat16)
    weight_grad = jnp.einsum('re,rtx->etx', encodings.astype(jnp.float32), block_grad_b.astype(jnp.float32), precision=lax.Precision.HIGHEST)
    return (attended, query_grad, encoding_grad, weight_grad)
```

```python
import jax
import jax.numpy as jnp
from jax import lax
from jax.experimental import pallas as pl
from jax.experimental.pallas import tpu as pltpu
from jax.sharding import Mesh
from jax.sharding import PartitionSpec as P

HD = 128
SPAN = 64
NROWS = 128
NBR = 2
NY = 4
NZ = 16
NC = 2
NX = 4
DP = ("y", "z", "c")
ENC = 896
OWN = 7
PAD = 8
COLS = 1024
HALF = NY * NZ * PAD
NT = (((1,), (1,)), ((), ()))
TN = (((0,), (0,)), ((), ()))
SLOT_OWN, SLOT_RIGHT, SLOT_LEFT, SLOT_SWAP, SLOT_CROSS = range(5)


def swap_cores(value):
    return lax.ppermute(value, "c", [(0, 1), (1, 0)])


def shifted(value, steps):
    count = NY * NZ * NC
    return lax.ppermute(value, DP, [(i, (i + steps) % count) for i in range(count)])


def crossed(value):
    count = NY * NZ * NC
    return lax.ppermute(
        value, DP, [(i, (i + (1 if i % 2 else -1)) % count) for i in range(count)]
    )


def spread(value, axis, count):
    return lax.all_to_all(
        jnp.broadcast_to(value[None], (count,) + value.shape), axis, 0, 0
    )


def natural_column(core):
    place = jnp.arange(NC * HALF, dtype=jnp.int32)
    row = place % PAD
    z = place // PAD % NZ
    y = place // (PAD * NZ) % NY
    c = (place // HALF + core) % NC
    return jnp.where(row < OWN, ((y * NZ + z) * NC + c) * OWN + row, -1)


def attention_kernel(
    sel_ref, core_ref, x_ref, xt_ref, wa_ref, wb_ref, q_ref, g_ref,
    att_ref, qg_ref, keep_ref, send_ref, ekeep_ref, kv_ref, cb_ref, acc_ref,
):
    f32, b16 = jnp.float32, jnp.bfloat16
    factor = 1.0 / HD**0.5
    kv = jnp.dot(x_ref[:, :HALF], wa_ref[...], preferred_element_type=f32)
    kv = kv + jnp.dot(x_ref[:, HALF:], wb_ref[...], preferred_element_type=f32)
    kv_ref[...] = kv.astype(b16)
    keys_here = NBR * NROWS
    heads = COLS // 2 // HD
    for span in range(2):
        rows = slice(span * SPAN, (span + 1) * SPAN)
        krows = slice(span * keys_here, (span + 1) * keys_here)
        for head in range(heads):
            kc = slice(head * HD, (head + 1) * HD)
            vc = slice((heads + head) * HD, (heads + head + 1) * HD)
            q, g = q_ref[rows, kc], g_ref[rows, kc]
            k, v = kv_ref[krows, kc], kv_ref[krows, vc]
            scores = lax.dot_general(q, k, NT, preferred_element_type=f32) * factor
            top = jnp.max(scores, axis=-1, keepdims=True)
            raised = jnp.exp(scores - top)
            probs = raised / jnp.sum(raised, axis=-1, keepdims=True)
            probs_b = probs.astype(b16)
            att_ref[rows, kc] = jnp.dot(probs_b, v, preferred_element_type=f32).astype(b16)
            dprobs = lax.dot_general(g, v, NT, preferred_element_type=f32)
            delta = jnp.sum(probs * dprobs, axis=-1, keepdims=True)
            dscores = (probs * (dprobs - delta) * factor).astype(b16)
            qg_ref[rows, kc] = jnp.dot(dscores, k, preferred_element_type=f32).astype(b16)
            kgrad = lax.dot_general(dscores, q, TN, preferred_element_type=f32)
            vgrad = lax.dot_general(probs_b, g, TN, preferred_element_type=f32)
            cb_ref[krows, kc] = kgrad.astype(b16)
            cb_ref[krows, vc] = vgrad.astype(b16)
    keep_ref[...] = jnp.dot(
        xt_ref[:HALF, :], cb_ref[...], preferred_element_type=f32
    ).astype(b16)
    send_ref[:HALF, :] = jnp.dot(
        xt_ref[HALF:, :], cb_ref[...], preferred_element_type=f32
    ).astype(b16)
    acc_ref[...] = jnp.zeros_like(acc_ref)
    core = core_ref[0]
    for half, w_ref in ((0, wa_ref), (1, wb_ref)):
        part = lax.dot_general(cb_ref[...], w_ref[...], NT, preferred_element_type=f32)
        c = (core + half) % NC
        for pair in range(2 * NBR):
            for y in range(NY):
                lanes = pl.ds(pl.multiple_of(y * 256 + c * 128, 128), 128)
                acc_ref[sel_ref[pair], :, lanes] += part[
                    pair * NROWS : (pair + 1) * NROWS, y * 128 : (y + 1) * 128
                ]
    for place in range(3):
        ekeep_ref[place * NROWS : (place + 1) * NROWS, :] = acc_ref[place].astype(b16)
    for place in range(2):
        send_ref[HALF + place * NROWS : HALF + (place + 1) * NROWS, :] = acc_ref[
            3 + place
        ].astype(b16)


def attend(sel, core, x, xt, wa, wb, q, g):
    b16 = jnp.bfloat16
    vmem = pl.BlockSpec(memory_space=pltpu.VMEM)
    smem = pl.BlockSpec(memory_space=pltpu.SMEM)
    return pl.pallas_call(
        attention_kernel,
        out_shape=(
            jax.ShapeDtypeStruct(q.shape, b16),
            jax.ShapeDtypeStruct(q.shape, b16),
            jax.ShapeDtypeStruct((HALF, COLS), b16),
            jax.ShapeDtypeStruct((HALF + 2 * NROWS, COLS), b16),
            jax.ShapeDtypeStruct((3 * NROWS, COLS), b16),
        ),
        in_specs=[smem, smem] + [vmem] * 6,
        out_specs=(vmem,) * 5,
        scratch_shapes=[
            pltpu.VMEM((4 * NROWS, COLS), b16),
            pltpu.VMEM((4 * NROWS, COLS), b16),
            pltpu.VMEM((5, NROWS, COLS), jnp.float32),
        ],
        compiler_params=pltpu.CompilerParams(vmem_limit_bytes=40 * 2**20),
        cost_estimate=pl.CostEstimate(
            flops=4_000_000_000, bytes_accessed=8_000_000, transcendentals=131072
        ),
    )(sel, core, x, xt, wa, wb, q, g)


def per_device(queries, encodings, kv_weight, pair_list, cotangent):
    f32, b16 = jnp.float32, jnp.bfloat16
    core = lax.axis_index("c")
    me = (lax.axis_index("y") * NZ + lax.axis_index("z")) * NC + core
    count = NY * NZ * NC

    shard = jnp.pad(kv_weight.reshape(OWN, COLS), ((0, PAD - OWN), (0, 0)))
    w = spread(shard, "z", NZ).reshape(NZ * PAD, COLS)
    w = spread(w, "y", NY).reshape(HALF, COLS)
    w_other = swap_cores(w)

    window = jnp.stack(
        [
            encodings,
            shifted(encodings, -2),
            shifted(encodings, 2),
            swap_cores(encodings),
            crossed(encodings),
        ]
    )
    offset = (pair_list.reshape(-1) - me + count) % count
    near = jnp.where(core == 0, 1, count - 1)
    sel = jnp.where(
        offset == 0,
        SLOT_OWN,
        jnp.where(
            offset == 2,
            SLOT_RIGHT,
            jnp.where(
                offset == count - 2,
                SLOT_LEFT,
                jnp.where(offset == near, SLOT_SWAP, SLOT_CROSS),
            ),
        ),
    ).astype(jnp.int32)
    chosen = jnp.take(window, sel, axis=0, mode="clip").reshape(4 * NROWS, ENC)
    column = natural_column(core)
    pick = (jnp.arange(ENC, dtype=jnp.int32)[:, None] == column[None, :]).astype(b16)
    x = jnp.dot(chosen, pick, preferred_element_type=f32).astype(b16)
    xt = lax.dot_general(pick, chosen, (((0,), (1,)), ((), ())), preferred_element_type=f32)
    xt = xt.astype(b16)

    attended, query_grad, keep, send, ekeep = attend(
        sel, core.reshape(1), x, xt, w, w_other, queries, cotangent
    )

    got = swap_cores(send)
    total = (keep.astype(f32) + got[:HALF].astype(f32)).astype(b16)
    parts = lax.all_to_all(total.reshape(NY, NZ * PAD, COLS), "y", 0, 0)
    total = jnp.sum(parts.astype(f32), axis=0).astype(b16)
    parts = lax.all_to_all(total.reshape(NZ, PAD, COLS), "z", 0, 0)
    weight_grad = jnp.sum(parts.astype(f32), axis=0)[:OWN].reshape(OWN, 2, COLS // 2)

    own = ekeep[:NROWS].astype(f32) + got[HALF : HALF + NROWS].astype(f32)
    cross = got[HALF + NROWS :].astype(f32)
    right = ekeep[NROWS : 2 * NROWS].astype(f32) + jnp.where(core == 0, cross, 0.0)
    left = ekeep[2 * NROWS :].astype(f32) + jnp.where(core == 1, cross, 0.0)
    from_left = shifted(right.astype(b16), 2)
    from_right = shifted(left.astype(b16), -2)
    mine = (own + from_left.astype(f32) + from_right.astype(f32)).astype(b16)
    mine = mine.reshape(NROWS, NX, COLS // NX).transpose(1, 0, 2)
    groups = lax.all_to_all(mine, "x", 0, 0)
    summed = jnp.sum(groups.astype(f32), axis=0).astype(b16)
    place = jnp.arange(COLS // NX, dtype=jnp.int32)
    row, z, c = place % PAD, place // PAD % NZ, place // (PAD * NZ)
    column = jnp.where(row < OWN, (z * NC + c) * OWN + row, -1)
    pick = (column[:, None] == jnp.arange(ENC // NX, dtype=jnp.int32)[None, :]).astype(b16)
    encoding_grad = jnp.dot(summed, pick, preferred_element_type=f32).astype(b16)
    return attended, query_grad, encoding_grad, weight_grad


def solution(mesh):
    mesh = Mesh(mesh.devices.reshape(NY, NZ, NC, NX), ("y", "z", "c", "x"))
    return jax.shard_map(
        per_device,
        mesh=mesh,
        in_specs=(P(DP, "x"), P(DP, None), P(DP, None, "x"), P(DP, None), P(DP, "x")),
        out_specs=(P(DP, "x"), P(DP, "x"), P(DP, "x"), P(DP, None, "x")),
        check_vma=False,
    )
```

```python
import jax
import jax.numpy as jnp
from jax import lax
from jax.experimental import pallas as pl
from jax.experimental.pallas import tpu as pltpu
from jax.sharding import Mesh
from jax.sharding import PartitionSpec as P

HD = 128
SPAN = 64
NROWS = 128
NBR = 2
NY = 4
NZ = 16
NC = 2
NX = 4
DP = ("y", "z", "c")
ENC = 896
OWN = 7
PAD = 8
COLS = 1024
HALF = NY * NZ * PAD
NT = (((1,), (1,)), ((), ()))
TN = (((0,), (0,)), ((), ()))
SLOT_OWN, SLOT_RIGHT, SLOT_LEFT, SLOT_SWAP, SLOT_CROSS = range(5)


def after(value, *earlier):
    return lax.optimization_barrier((value,) + earlier)[0]


def swap_cores(value):
    return lax.ppermute(value, "c", [(0, 1), (1, 0)])


def shifted(value, steps):
    count = NY * NZ * NC
    return lax.ppermute(value, DP, [(i, (i + steps) % count) for i in range(count)])


def crossed(value):
    count = NY * NZ * NC
    return lax.ppermute(
        value, DP, [(i, (i + (1 if i % 2 else -1)) % count) for i in range(count)]
    )


def natural_column(place, core):
    row = place % PAD
    z = place // PAD % NZ
    y = place // (PAD * NZ) % NY
    c = (place // HALF + core) % NC
    return jnp.where(row < OWN, ((y * NZ + z) * NC + c) * OWN + row, -1)


def select_kernel(
    sel_ref, core_ref, own_ref, right_ref, left_ref, other_ref, x_ref, xt_ref, chosen_ref
):
    f32, b16 = jnp.float32, jnp.bfloat16
    sources = (own_ref, right_ref, left_ref, other_ref, other_ref)
    for pair in range(2 * NBR):
        for slot, source in enumerate(sources):
            first = NROWS if slot == SLOT_CROSS else 0

            @pl.when(sel_ref[pair] == slot)
            def _():
                chosen_ref[pair * NROWS : (pair + 1) * NROWS, :] = source[
                    first : first + NROWS, :
                ]

    place = lax.broadcasted_iota(jnp.int32, (1, NC * HALF), 1)
    column = natural_column(place, core_ref[0])
    pick = lax.broadcasted_iota(jnp.int32, (ENC, NC * HALF), 0) == column
    pick = jnp.where(pick, 1.0, 0.0).astype(b16)
    x = jnp.dot(chosen_ref[...], pick, preferred_element_type=f32)
    x_ref[...] = x.astype(b16)
    xt_ref[...] = x.T.astype(b16)


def select(sel, core, own, right, left, other):
    b16 = jnp.bfloat16
    vmem = pl.BlockSpec(memory_space=pltpu.VMEM)
    smem = pl.BlockSpec(memory_space=pltpu.SMEM)
    return pl.pallas_call(
        select_kernel,
        out_shape=(
            jax.ShapeDtypeStruct((4 * NROWS, COLS), b16),
            jax.ShapeDtypeStruct((COLS, 4 * NROWS), b16),
        ),
        in_specs=[smem, smem] + [vmem] * 4,
        out_specs=(vmem,) * 2,
        scratch_shapes=[pltpu.VMEM((4 * NROWS, ENC), b16)],
        compiler_params=pltpu.CompilerParams(vmem_limit_bytes=16 * 2**20),
        cost_estimate=pl.CostEstimate(
            flops=1_000_000_000, bytes_accessed=3_000_000, transcendentals=0
        ),
    )(sel, core, own, right, left, other)


def attention_kernel(
    x_ref, xt_ref, wa_ref, wb_ref, q_ref, g_ref, att_ref, qg_ref, cb_ref, send_ref, kv_ref
):
    f32, b16 = jnp.float32, jnp.bfloat16
    factor = 1.0 / HD**0.5
    kv = jnp.dot(x_ref[:, :HALF], wa_ref[...], preferred_element_type=f32)
    kv = kv + jnp.dot(x_ref[:, HALF:], wb_ref[...], preferred_element_type=f32)
    kv_ref[...] = kv.astype(b16)
    heads = COLS // 2 // HD
    units = [(span, head) for span in range(2) for head in range(heads)]
    rows = [slice(span * SPAN, (span + 1) * SPAN) for span, _ in units]
    span_rows = NBR * NROWS
    krows = [slice(span * span_rows, (span + 1) * span_rows) for span, _ in units]
    kcols = [slice(head * HD, (head + 1) * HD) for _, head in units]
    vcols = [slice((heads + head) * HD, (heads + head + 1) * HD) for _, head in units]
    q = [q_ref[r, c] for r, c in zip(rows, kcols)]
    g = [g_ref[r, c] for r, c in zip(rows, kcols)]
    k = [kv_ref[r, c] for r, c in zip(krows, kcols)]
    v = [kv_ref[r, c] for r, c in zip(krows, vcols)]
    scores = [
        lax.dot_general(a, b, NT, preferred_element_type=f32) * factor for a, b in zip(q, k)
    ]
    dprobs = [lax.dot_general(a, b, NT, preferred_element_type=f32) for a, b in zip(g, v)]
    raised = [jnp.exp(a - jnp.max(a, axis=-1, keepdims=True)) for a in scores]
    probs = [a / jnp.sum(a, axis=-1, keepdims=True) for a in raised]
    probs_b = [a.astype(b16) for a in probs]
    delta = [jnp.sum(a * b, axis=-1, keepdims=True) for a, b in zip(probs, dprobs)]
    dscores = [
        (a * (b - c) * factor).astype(b16) for a, b, c in zip(probs, dprobs, delta)
    ]
    for i in range(len(units)):
        out = jnp.dot(probs_b[i], v[i], preferred_element_type=f32)
        att_ref[rows[i], kcols[i]] = out.astype(b16)
    for i in range(len(units)):
        vgrad = lax.dot_general(probs_b[i], g[i], TN, preferred_element_type=f32)
        cb_ref[krows[i], vcols[i]] = vgrad.astype(b16)
    for i in range(len(units)):
        out = jnp.dot(dscores[i], k[i], preferred_element_type=f32)
        qg_ref[rows[i], kcols[i]] = out.astype(b16)
    for i in range(len(units)):
        kgrad = lax.dot_general(dscores[i], q[i], TN, preferred_element_type=f32)
        cb_ref[krows[i], kcols[i]] = kgrad.astype(b16)
    send_ref[...] = jnp.dot(
        xt_ref[HALF:, :], cb_ref[...], preferred_element_type=f32
    ).astype(b16)


def attend(x, xt, wa, wb, q, g):
    b16 = jnp.bfloat16
    vmem = pl.BlockSpec(memory_space=pltpu.VMEM)
    pairs = jax.ShapeDtypeStruct((4 * NROWS, COLS), b16)
    return pl.pallas_call(
        attention_kernel,
        out_shape=(
            jax.ShapeDtypeStruct(q.shape, b16),
            jax.ShapeDtypeStruct(q.shape, b16),
            pairs,
            jax.ShapeDtypeStruct((HALF, COLS), b16),
        ),
        in_specs=[vmem] * 6,
        out_specs=(vmem,) * 4,
        scratch_shapes=[pltpu.VMEM(pairs.shape, b16)],
        compiler_params=pltpu.CompilerParams(vmem_limit_bytes=20 * 2**20),
        cost_estimate=pl.CostEstimate(
            flops=2_500_000_000, bytes_accessed=6_000_000, transcendentals=131072
        ),
    )(x, xt, wa, wb, q, g)


def share_kernel(
    sel_ref, core_ref, xt_ref, wa_ref, wb_ref, cb_ref, keep_ref, ekeep_ref, esend_ref, acc_ref
):
    f32, b16 = jnp.float32, jnp.bfloat16
    keep_ref[...] = jnp.dot(
        xt_ref[:HALF, :], cb_ref[...], preferred_element_type=f32
    ).astype(b16)
    acc_ref[...] = jnp.zeros_like(acc_ref)
    core = core_ref[0]
    for half, w_ref in ((0, wa_ref), (1, wb_ref)):
        part = lax.dot_general(cb_ref[...], w_ref[...], NT, preferred_element_type=f32)
        c = (core + half) % NC
        for pair in range(2 * NBR):
            for y in range(NY):
                lanes = pl.ds(pl.multiple_of(y * 256 + c * 128, 128), 128)
                acc_ref[sel_ref[pair], :, lanes] += part[
                    pair * NROWS : (pair + 1) * NROWS, y * 128 : (y + 1) * 128
                ]
    for place in range(3):
        ekeep_ref[place * NROWS : (place + 1) * NROWS, :] = acc_ref[place].astype(b16)
    for place in range(2):
        esend_ref[place * NROWS : (place + 1) * NROWS, :] = acc_ref[3 + place].astype(b16)


def share(sel, core, xt, wa, wb, contributions):
    b16 = jnp.bfloat16
    vmem = pl.BlockSpec(memory_space=pltpu.VMEM)
    smem = pl.BlockSpec(memory_space=pltpu.SMEM)
    return pl.pallas_call(
        share_kernel,
        out_shape=(
            jax.ShapeDtypeStruct((HALF, COLS), b16),
            jax.ShapeDtypeStruct((3 * NROWS, COLS), b16),
            jax.ShapeDtypeStruct((2 * NROWS, COLS), b16),
        ),
        in_specs=[smem, smem] + [vmem] * 4,
        out_specs=(vmem,) * 3,
        scratch_shapes=[pltpu.VMEM((5, NROWS, COLS), jnp.float32)],
        compiler_params=pltpu.CompilerParams(vmem_limit_bytes=16 * 2**20),
        cost_estimate=pl.CostEstimate(
            flops=1_600_000_000, bytes_accessed=6_000_000, transcendentals=0
        ),
    )(sel, core, xt, wa, wb, contributions)


def merge_kernel(core_ref, x_ref, keep_ref, got_ref, *out_refs):
    f32 = jnp.float32
    from_cross = (None, core_ref[0] == 0, core_ref[0] == 1)
    for step, out_ref in enumerate(out_refs):
        part = (x_ref[0] + step) % NX
        lanes = pl.ds(pl.multiple_of(part * out_ref.shape[1], 128), out_ref.shape[1])
        swap = got_ref[:NROWS, lanes].astype(f32)
        cross = got_ref[NROWS:, lanes].astype(f32)
        for slot in (SLOT_OWN, SLOT_RIGHT, SLOT_LEFT):
            rows = slice(slot * NROWS, (slot + 1) * NROWS)
            total = keep_ref[rows, lanes].astype(f32)
            if slot == SLOT_OWN:
                total = total + swap
            else:
                total = total + jnp.where(from_cross[slot], cross, 0.0)
            out_ref[rows, :] = total.astype(out_ref.dtype)


def small_call(kernel, scalars, arrays, outs):
    vmem = pl.BlockSpec(memory_space=pltpu.VMEM)
    smem = pl.BlockSpec(memory_space=pltpu.SMEM)
    return pl.pallas_call(
        kernel,
        out_shape=outs,
        in_specs=[smem] * len(scalars) + [vmem] * len(arrays),
        out_specs=(vmem,) * len(outs),
        compiler_params=pltpu.CompilerParams(vmem_limit_bytes=8 * 2**20),
        cost_estimate=pl.CostEstimate(flops=1000, bytes_accessed=1000, transcendentals=0),
    )(*scalars, *arrays)


def summed(refs, rows):
    total = refs[0][rows, :].astype(jnp.float32)
    for ref in refs[1:]:
        total = total + ref[rows, :].astype(jnp.float32)
    return total


def groups_kernel(a_ref, b_ref, c_ref, d_ref, *out_refs):
    for slot, out_ref in enumerate(out_refs):
        rows = slice(slot * NROWS, (slot + 1) * NROWS)
        out_ref[...] = summed((a_ref, b_ref, c_ref, d_ref), rows).astype(out_ref.dtype)


def spread_kernel(w_ref, out_ref):
    f32 = jnp.float32
    half = COLS // 2
    left = [w_ref[r][:1, :].astype(f32) for r in range(OWN)]
    right = [w_ref[r][1:, :].astype(f32) for r in range(OWN)]
    blank = [jnp.zeros((PAD - OWN, half), f32)]
    rows = [jnp.concatenate(side + blank, axis=0) for side in (left, right)]
    rows = jnp.concatenate(rows, axis=1).astype(out_ref.dtype)
    for copy in range(out_ref.shape[0]):
        out_ref[copy] = rows


def reduced_kernel(parts_ref, out_ref):
    total = parts_ref[0].astype(jnp.float32)
    for i in range(1, parts_ref.shape[0]):
        total = total + parts_ref[i].astype(jnp.float32)
    out_ref[...] = total.astype(out_ref.dtype)


def reduced(parts):
    out = jax.ShapeDtypeStruct(parts.shape[1:], parts.dtype)
    return small_call(reduced_kernel, (), (parts,), (out,))[0]


def finish_kernel(own_ref, left_ref, right_ref, out_ref):
    b16 = jnp.bfloat16
    total = summed((own_ref, left_ref, right_ref), slice(None)).astype(b16)
    width, size = out_ref.shape[0], total.shape[1]
    place = lax.broadcasted_iota(jnp.int32, (1, size), 1)
    row, z, c = place % PAD, place // PAD % NZ, place // (PAD * NZ)
    column = jnp.where(row < OWN, (z * NC + c) * OWN + row, -1)
    pick = lax.broadcasted_iota(jnp.int32, (width, size), 0) == column
    pick = jnp.where(pick, 1.0, 0.0).astype(b16)
    out_ref[...] = lax.dot_general(
        pick, total, NT, preferred_element_type=jnp.float32
    ).astype(b16)


def per_device(queries, encodings, kv_weight, pair_list, cotangent):
    f32, b16 = jnp.float32, jnp.bfloat16
    core = lax.axis_index("c")
    me = (lax.axis_index("y") * NZ + lax.axis_index("z")) * NC + core
    count = NY * NZ * NC

    right = shifted(encodings, -2)
    left = shifted(encodings, 2)
    copies = jax.ShapeDtypeStruct((NZ, PAD, COLS), b16)
    (copies,) = small_call(spread_kernel, (), (kv_weight,), (copies,))
    w = lax.all_to_all(copies, "z", 0, 0).reshape(NZ * PAD, COLS)
    copies = jnp.broadcast_to(w[None], (NY,) + w.shape)
    here = after(encodings, copies)
    w = lax.all_to_all(copies, "y", 0, 0).reshape(HALF, COLS)
    other = swap_cores(jnp.concatenate([here, jnp.where(core == 0, right, left)]))

    offset = (pair_list.reshape(-1) - me + count) % count
    near = jnp.where(core == 0, 1, count - 1)
    sel = jnp.where(
        offset == 0,
        SLOT_OWN,
        jnp.where(
            offset == 2,
            SLOT_RIGHT,
            jnp.where(
                offset == count - 2,
                SLOT_LEFT,
                jnp.where(offset == near, SLOT_SWAP, SLOT_CROSS),
            ),
        ),
    ).astype(jnp.int32)
    w, other = lax.optimization_barrier((w, other))
    w_other = swap_cores(w)
    core_id = core.reshape(1)
    x, xt = select(sel, core_id, encodings, right, left, other)

    attended, query_grad, contributions, send = attend(
        x, xt, w, w_other, queries, cotangent
    )
    got = swap_cores(send)
    keep, ekeep, esend = share(sel, core_id, xt, w, w_other, contributions)
    total = (keep.astype(f32) + got.astype(f32)).astype(b16)
    esend = after(esend, total)
    parts = lax.all_to_all(total.reshape(NY, NZ * PAD, COLS), "y", 0, 0)
    got = swap_cores(esend)

    part = jax.ShapeDtypeStruct((3 * NROWS, COLS // NX), b16)
    slot = jax.ShapeDtypeStruct((NROWS, COLS // NX), b16)
    x_id = lax.axis_index("x").reshape(1)
    groups = list(small_call(merge_kernel, (core_id, x_id), (ekeep, got), (part,) * NX))
    for step in range(1, NX):
        groups[step] = lax.ppermute(
            groups[step], "x", [(i, (i + step) % NX) for i in range(NX)]
        )
    total = reduced(after(parts, groups[1], groups[2]))
    groups[0] = after(groups[0], total)
    parts = lax.all_to_all(total.reshape(NZ, PAD, COLS), "z", 0, 0)
    weight_grad = jnp.sum(parts.astype(f32), axis=0)[:OWN].reshape(OWN, 2, COLS // 2)
    own, right, left = small_call(groups_kernel, (), groups, (slot,) * 3)
    from_left = shifted(right, 2)
    from_right = shifted(left, -2)
    flipped = jax.ShapeDtypeStruct((ENC // NX, NROWS), b16)
    (flipped,) = small_call(finish_kernel, (), (own, from_left, from_right), (flipped,))
    encoding_grad = flipped.T
    return attended, query_grad, encoding_grad, weight_grad


def solution(mesh):
    mesh = Mesh(mesh.devices.reshape(NY, NZ, NC, NX), ("y", "z", "c", "x"))
    return jax.shard_map(
        per_device,
        mesh=mesh,
        in_specs=(P(DP, "x"), P(DP, None), P(DP, None, "x"), P(DP, None), P(DP, "x")),
        out_specs=(P(DP, "x"), P(DP, "x"), P(DP, "x"), P(DP, None, "x")),
        check_vma=False,
    )
```

```python
import jax
import jax.numpy as jnp
from jax import lax
from jax.experimental import pallas as pl
from jax.experimental.pallas import tpu as pltpu
from jax.sharding import Mesh
from jax.sharding import PartitionSpec as P

HD = 128
SPAN = 64
NROWS = 128
NBR = 2
NY = 4
NZ = 16
NC = 2
NX = 4
DP = ("y", "z", "c")
ENC = 896
OWN = 7
PAD = 8
COLS = 1024
HALF = NY * NZ * PAD
NT = (((1,), (1,)), ((), ()))
TN = (((0,), (0,)), ((), ()))
SLOT_OWN, SLOT_RIGHT, SLOT_LEFT, SLOT_SWAP, SLOT_CROSS = range(5)


def after(value, *earlier):
    return lax.optimization_barrier((value,) + earlier)[0]


def swap_cores(value):
    return lax.ppermute(value, "c", [(0, 1), (1, 0)])


def shifted(value, steps):
    count = NY * NZ * NC
    return lax.ppermute(value, DP, [(i, (i + steps) % count) for i in range(count)])


def crossed(value):
    count = NY * NZ * NC
    return lax.ppermute(
        value, DP, [(i, (i + (1 if i % 2 else -1)) % count) for i in range(count)]
    )


def natural_column(place, core):
    row = place % PAD
    z = place // PAD % NZ
    y = place // (PAD * NZ) % NY
    c = (place // HALF + core) % NC
    return jnp.where(row < OWN, ((y * NZ + z) * NC + c) * OWN + row, -1)


def select_kernel(
    sel_ref, core_ref, own_ref, right_ref, left_ref, other_ref, x_ref, xt_ref, chosen_ref
):
    f32, b16 = jnp.float32, jnp.bfloat16
    sources = (own_ref, right_ref, left_ref, other_ref, other_ref)
    for pair in range(2 * NBR):
        for slot, source in enumerate(sources):
            first = NROWS if slot == SLOT_CROSS else 0

            @pl.when(sel_ref[pair] == slot)
            def _():
                chosen_ref[pair * NROWS : (pair + 1) * NROWS, :] = source[
                    first : first + NROWS, :
                ]

    place = lax.broadcasted_iota(jnp.int32, (1, NC * HALF), 1)
    column = natural_column(place, core_ref[0])
    pick = lax.broadcasted_iota(jnp.int32, (ENC, NC * HALF), 0) == column
    pick = jnp.where(pick, 1.0, 0.0).astype(b16)
    x = jnp.dot(chosen_ref[...], pick, preferred_element_type=f32)
    x_ref[...] = x.astype(b16)
    xt_ref[...] = x.T.astype(b16)


def select(sel, core, own, right, left, other):
    b16 = jnp.bfloat16
    vmem = pl.BlockSpec(memory_space=pltpu.VMEM)
    smem = pl.BlockSpec(memory_space=pltpu.SMEM)
    return pl.pallas_call(
        select_kernel,
        out_shape=(
            jax.ShapeDtypeStruct((4 * NROWS, COLS), b16),
            jax.ShapeDtypeStruct((COLS, 4 * NROWS), b16),
        ),
        in_specs=[smem, smem] + [vmem] * 4,
        out_specs=(vmem,) * 2,
        scratch_shapes=[pltpu.VMEM((4 * NROWS, ENC), b16)],
        compiler_params=pltpu.CompilerParams(vmem_limit_bytes=16 * 2**20),
        cost_estimate=pl.CostEstimate(
            flops=1_000_000_000, bytes_accessed=3_000_000, transcendentals=0
        ),
    )(sel, core, own, right, left, other)


def project_kernel(x_ref, w_ref, kv_ref):
    kv_ref[...] = jnp.dot(x_ref[:, :HALF], w_ref[...], preferred_element_type=jnp.float32)


def attention_kernel(
    x_ref, xt_ref, part_ref, wb_ref, q_ref, g_ref, att_ref, qg_ref, cb_ref, send_ref, kv_ref
):
    f32, b16 = jnp.float32, jnp.bfloat16
    factor = 1.0 / HD**0.5
    kv = part_ref[...] + jnp.dot(x_ref[:, HALF:], wb_ref[...], preferred_element_type=f32)
    kv_ref[...] = kv.astype(b16)
    heads = COLS // 2 // HD
    units = [(span, head) for span in range(2) for head in range(heads)]
    rows = [slice(span * SPAN, (span + 1) * SPAN) for span, _ in units]
    span_rows = NBR * NROWS
    krows = [slice(span * span_rows, (span + 1) * span_rows) for span, _ in units]
    kcols = [slice(head * HD, (head + 1) * HD) for _, head in units]
    vcols = [slice((heads + head) * HD, (heads + head + 1) * HD) for _, head in units]
    q = [q_ref[r, c] for r, c in zip(rows, kcols)]
    g = [g_ref[r, c] for r, c in zip(rows, kcols)]
    k = [kv_ref[r, c] for r, c in zip(krows, kcols)]
    v = [kv_ref[r, c] for r, c in zip(krows, vcols)]
    scores = [
        lax.dot_general(a, b, NT, preferred_element_type=f32) * factor for a, b in zip(q, k)
    ]
    dprobs = [lax.dot_general(a, b, NT, preferred_element_type=f32) for a, b in zip(g, v)]
    raised = [jnp.exp(a - jnp.max(a, axis=-1, keepdims=True)) for a in scores]
    probs = [a / jnp.sum(a, axis=-1, keepdims=True) for a in raised]
    probs_b = [a.astype(b16) for a in probs]
    delta = [jnp.sum(a * b, axis=-1, keepdims=True) for a, b in zip(probs, dprobs)]
    dscores = [
        (a * (b - c) * factor).astype(b16) for a, b, c in zip(probs, dprobs, delta)
    ]
    for i in range(len(units)):
        out = jnp.dot(probs_b[i], v[i], preferred_element_type=f32)
        att_ref[rows[i], kcols[i]] = out.astype(b16)
    for i in range(len(units)):
        vgrad = lax.dot_general(probs_b[i], g[i], TN, preferred_element_type=f32)
        cb_ref[krows[i], vcols[i]] = vgrad.astype(b16)
    for i in range(len(units)):
        out = jnp.dot(dscores[i], k[i], preferred_element_type=f32)
        qg_ref[rows[i], kcols[i]] = out.astype(b16)
    for i in range(len(units)):
        kgrad = lax.dot_general(dscores[i], q[i], TN, preferred_element_type=f32)
        cb_ref[krows[i], kcols[i]] = kgrad.astype(b16)
    send_ref[...] = jnp.dot(
        xt_ref[HALF:, :], cb_ref[...], preferred_element_type=f32
    ).astype(b16)


def attend(x, xt, part, wb, q, g):
    b16 = jnp.bfloat16
    vmem = pl.BlockSpec(memory_space=pltpu.VMEM)
    pairs = jax.ShapeDtypeStruct((4 * NROWS, COLS), b16)
    return pl.pallas_call(
        attention_kernel,
        out_shape=(
            jax.ShapeDtypeStruct(q.shape, b16),
            jax.ShapeDtypeStruct(q.shape, b16),
            pairs,
            jax.ShapeDtypeStruct((HALF, COLS), b16),
        ),
        in_specs=[vmem] * 6,
        out_specs=(vmem,) * 4,
        scratch_shapes=[pltpu.VMEM(pairs.shape, b16)],
        compiler_params=pltpu.CompilerParams(vmem_limit_bytes=20 * 2**20),
        cost_estimate=pl.CostEstimate(
            flops=2_500_000_000, bytes_accessed=6_000_000, transcendentals=131072
        ),
    )(x, xt, part, wb, q, g)


def share_kernel(
    sel_ref, core_ref, xt_ref, wa_ref, wb_ref, cb_ref, keep_ref, ekeep_ref, esend_ref, acc_ref
):
    f32, b16 = jnp.float32, jnp.bfloat16
    keep_ref[...] = jnp.dot(
        xt_ref[:HALF, :], cb_ref[...], preferred_element_type=f32
    ).astype(b16)
    acc_ref[...] = jnp.zeros_like(acc_ref)
    core = core_ref[0]
    for half, w_ref in ((0, wa_ref), (1, wb_ref)):
        part = lax.dot_general(cb_ref[...], w_ref[...], NT, preferred_element_type=f32)
        c = (core + half) % NC
        for pair in range(2 * NBR):
            for y in range(NY):
                lanes = pl.ds(pl.multiple_of(y * 256 + c * 128, 128), 128)
                acc_ref[sel_ref[pair], :, lanes] += part[
                    pair * NROWS : (pair + 1) * NROWS, y * 128 : (y + 1) * 128
                ]
    for place in range(3):
        ekeep_ref[place * NROWS : (place + 1) * NROWS, :] = acc_ref[place].astype(b16)
    for place in range(2):
        esend_ref[place * NROWS : (place + 1) * NROWS, :] = acc_ref[3 + place].astype(b16)


def share(sel, core, xt, wa, wb, contributions):
    b16 = jnp.bfloat16
    vmem = pl.BlockSpec(memory_space=pltpu.VMEM)
    smem = pl.BlockSpec(memory_space=pltpu.SMEM)
    return pl.pallas_call(
        share_kernel,
        out_shape=(
            jax.ShapeDtypeStruct((HALF, COLS), b16),
            jax.ShapeDtypeStruct((3 * NROWS, COLS), b16),
            jax.ShapeDtypeStruct((2 * NROWS, COLS), b16),
        ),
        in_specs=[smem, smem] + [vmem] * 4,
        out_specs=(vmem,) * 3,
        scratch_shapes=[pltpu.VMEM((5, NROWS, COLS), jnp.float32)],
        compiler_params=pltpu.CompilerParams(vmem_limit_bytes=16 * 2**20),
        cost_estimate=pl.CostEstimate(
            flops=1_600_000_000, bytes_accessed=6_000_000, transcendentals=0
        ),
    )(sel, core, xt, wa, wb, contributions)


def merge_kernel(core_ref, x_ref, keep_ref, got_ref, *out_refs):
    f32 = jnp.float32
    from_cross = (None, core_ref[0] == 0, core_ref[0] == 1)
    for step, out_ref in enumerate(out_refs):
        part = (x_ref[0] + step) % NX
        lanes = pl.ds(pl.multiple_of(part * out_ref.shape[1], 128), out_ref.shape[1])
        swap = got_ref[:NROWS, lanes].astype(f32)
        cross = got_ref[NROWS:, lanes].astype(f32)
        for slot in (SLOT_OWN, SLOT_RIGHT, SLOT_LEFT):
            rows = slice(slot * NROWS, (slot + 1) * NROWS)
            total = keep_ref[rows, lanes].astype(f32)
            if slot == SLOT_OWN:
                total = total + swap
            else:
                total = total + jnp.where(from_cross[slot], cross, 0.0)
            out_ref[rows, :] = total.astype(out_ref.dtype)


def small_call(kernel, scalars, arrays, outs):
    vmem = pl.BlockSpec(memory_space=pltpu.VMEM)
    smem = pl.BlockSpec(memory_space=pltpu.SMEM)
    return pl.pallas_call(
        kernel,
        out_shape=outs,
        in_specs=[smem] * len(scalars) + [vmem] * len(arrays),
        out_specs=(vmem,) * len(outs),
        compiler_params=pltpu.CompilerParams(vmem_limit_bytes=8 * 2**20),
        cost_estimate=pl.CostEstimate(flops=1000, bytes_accessed=1000, transcendentals=0),
    )(*scalars, *arrays)


def summed(refs, rows):
    total = refs[0][rows, :].astype(jnp.float32)
    for ref in refs[1:]:
        total = total + ref[rows, :].astype(jnp.float32)
    return total


def groups_kernel(a_ref, b_ref, c_ref, d_ref, *out_refs):
    for slot, out_ref in enumerate(out_refs):
        rows = slice(slot * NROWS, (slot + 1) * NROWS)
        out_ref[...] = summed((a_ref, b_ref, c_ref, d_ref), rows).astype(out_ref.dtype)


def spread_kernel(w_ref, out_ref):
    f32 = jnp.float32
    half = COLS // 2
    left = [w_ref[r][:1, :].astype(f32) for r in range(OWN)]
    right = [w_ref[r][1:, :].astype(f32) for r in range(OWN)]
    blank = [jnp.zeros((PAD - OWN, half), f32)]
    rows = [jnp.concatenate(side + blank, axis=0) for side in (left, right)]
    rows = jnp.concatenate(rows, axis=1).astype(out_ref.dtype)
    for copy in range(out_ref.shape[0]):
        out_ref[copy] = rows


def reduced_kernel(parts_ref, out_ref):
    total = parts_ref[0].astype(jnp.float32)
    for i in range(1, parts_ref.shape[0]):
        total = total + parts_ref[i].astype(jnp.float32)
    out_ref[...] = total.astype(out_ref.dtype)


def reduced(parts):
    out = jax.ShapeDtypeStruct(parts.shape[1:], parts.dtype)
    return small_call(reduced_kernel, (), (parts,), (out,))[0]


def add_kernel(keep_ref, got_ref, out_ref, sum_ref, sems):
    copies = []
    for part in range(NY):
        size = sum_ref.shape[1]
        rows = slice(part * size, (part + 1) * size)
        total = keep_ref[rows, :].astype(jnp.float32) + got_ref[rows, :].astype(jnp.float32)
        sum_ref[part] = total.astype(sum_ref.dtype)
        copies.append(pltpu.make_async_copy(sum_ref.at[part], out_ref.at[part], sems.at[part]))
        copies[-1].start()
    for copy in copies:
        copy.wait()


def copies_kernel(block_ref, out_ref, sems):
    copies = [
        pltpu.make_async_copy(block_ref, out_ref.at[i], sems.at[i])
        for i in range(out_ref.shape[0])
    ]
    for copy in copies:
        copy.start()
    for copy in copies:
        copy.wait()


def streamed(kernel, arrays, out, *scratch):
    vmem = pl.BlockSpec(memory_space=pltpu.VMEM)
    return pl.pallas_call(
        kernel,
        out_shape=out,
        in_specs=[vmem] * len(arrays),
        out_specs=pl.BlockSpec(memory_space=pl.ANY),
        scratch_shapes=list(scratch) + [pltpu.SemaphoreType.DMA((out.shape[0],))],
        compiler_params=pltpu.CompilerParams(vmem_limit_bytes=8 * 2**20),
        cost_estimate=pl.CostEstimate(flops=1000, bytes_accessed=1000, transcendentals=0),
    )(*arrays)


def finish_kernel(own_ref, left_ref, right_ref, out_ref):
    b16 = jnp.bfloat16
    total = summed((own_ref, left_ref, right_ref), slice(None)).astype(b16)
    width, size = out_ref.shape[0], total.shape[1]
    place = lax.broadcasted_iota(jnp.int32, (1, size), 1)
    row, z, c = place % PAD, place // PAD % NZ, place // (PAD * NZ)
    column = jnp.where(row < OWN, (z * NC + c) * OWN + row, -1)
    pick = lax.broadcasted_iota(jnp.int32, (width, size), 0) == column
    pick = jnp.where(pick, 1.0, 0.0).astype(b16)
    out_ref[...] = lax.dot_general(
        pick, total, NT, preferred_element_type=jnp.float32
    ).astype(b16)


def per_device(queries, encodings, kv_weight, pair_list, cotangent):
    f32, b16 = jnp.float32, jnp.bfloat16
    core = lax.axis_index("c")
    me = (lax.axis_index("y") * NZ + lax.axis_index("z")) * NC + core
    count = NY * NZ * NC

    right = shifted(encodings, -2)
    left = shifted(encodings, 2)
    copies = jax.ShapeDtypeStruct((NZ, PAD, COLS), b16)
    (copies,) = small_call(spread_kernel, (), (kv_weight,), (copies,))
    w = lax.all_to_all(copies, "z", 0, 0).reshape(NZ * PAD, COLS)
    copies = jax.ShapeDtypeStruct((NY,) + w.shape, b16)
    copies = streamed(copies_kernel, (w,), copies)
    here = after(encodings, copies)
    w = lax.all_to_all(copies, "y", 0, 0).reshape(HALF, COLS)
    other = swap_cores(jnp.concatenate([here, jnp.where(core == 0, right, left)]))

    offset = (pair_list.reshape(-1) - me + count) % count
    near = jnp.where(core == 0, 1, count - 1)
    sel = jnp.where(
        offset == 0,
        SLOT_OWN,
        jnp.where(
            offset == 2,
            SLOT_RIGHT,
            jnp.where(
                offset == count - 2,
                SLOT_LEFT,
                jnp.where(offset == near, SLOT_SWAP, SLOT_CROSS),
            ),
        ),
    ).astype(jnp.int32)
    core_id = core.reshape(1)
    x, xt = select(sel, core_id, encodings, right, left, other)
    w_other = swap_cores(after(w, x))
    part = jax.ShapeDtypeStruct((4 * NROWS, COLS), f32)
    (part,) = small_call(project_kernel, (), (x, w), (part,))

    attended, query_grad, contributions, send = attend(
        x, xt, part, w_other, queries, cotangent
    )
    got = swap_cores(send)
    keep, ekeep, esend = share(sel, core_id, xt, w, w_other, contributions)
    total = jax.ShapeDtypeStruct((NY, HALF // NY, COLS), b16)
    total = streamed(add_kernel, (keep, got), total, pltpu.VMEM(total.shape, b16))
    esend = after(esend, total)
    parts = lax.all_to_all(total, "y", 0, 0)
    got = swap_cores(esend)

    part = jax.ShapeDtypeStruct((3 * NROWS, COLS // NX), b16)
    slot = jax.ShapeDtypeStruct((NROWS, COLS // NX), b16)
    x_id = lax.axis_index("x").reshape(1)
    groups = list(small_call(merge_kernel, (core_id, x_id), (ekeep, got), (part,) * NX))
    for step in (2, 1, 3):
        groups[step] = lax.ppermute(
            groups[step], "x", [(i, (i + step) % NX) for i in range(NX)]
        )
    total = reduced(after(parts, groups[1], groups[3]))
    groups[0] = after(groups[0], total)
    parts = lax.all_to_all(total.reshape(NZ, PAD, COLS), "z", 0, 0)
    weight_grad = jnp.sum(parts.astype(f32), axis=0)[:OWN].reshape(OWN, 2, COLS // 2)
    own, right, left = small_call(groups_kernel, (), groups, (slot,) * 3)
    from_left = shifted(right, 2)
    from_right = shifted(left, -2)
    flipped = jax.ShapeDtypeStruct((ENC // NX, NROWS), b16)
    (flipped,) = small_call(finish_kernel, (), (own, from_left, from_right), (flipped,))
    encoding_grad = flipped.T
    return attended, query_grad, encoding_grad, weight_grad


def solution(mesh):
    mesh = Mesh(mesh.devices.reshape(NY, NZ, NC, NX), ("y", "z", "c", "x"))
    return jax.shard_map(
        per_device,
        mesh=mesh,
        in_specs=(P(DP, "x"), P(DP, None), P(DP, None, "x"), P(DP, None), P(DP, "x")),
        out_specs=(P(DP, "x"), P(DP, "x"), P(DP, "x"), P(DP, None, "x")),
        check_vma=False,
    )
```

```python
import jax
import jax.numpy as jnp
from jax import lax
from jax.experimental import pallas as pl
from jax.experimental.pallas import tpu as pltpu
from jax.sharding import Mesh
from jax.sharding import PartitionSpec as P

HD = 128
SPAN = 64
NROWS = 128
NBR = 2
NY = 4
NZ = 16
NC = 2
NX = 4
DP = ("y", "z", "c")
ENC = 896
OWN = 7
PAD = 8
COLS = 1024
SIDE = COLS // NC
PART = COLS // (2 * NC)
ROWS = NY * NZ * NC * PAD
NEAR = 6
NT = (((1,), (1,)), ((), ()))
TN = (((0,), (0,)), ((), ()))
OWN_BLOCK, RIGHT, LEFT = range(3)


def after(value, *earlier):
    return lax.optimization_barrier((value,) + earlier)[0]


def swap_cores(value):
    return lax.ppermute(value, "c", [(0, 1), (1, 0)])


def shifted(value, steps):
    count = NY * NZ * NC
    return lax.ppermute(value, DP, [(i, (i + steps) % count) for i in range(count)])


def natural_column(place):
    row = place % PAD
    return jnp.where(row < OWN, place // PAD * OWN + row, -1)


def small_call(kernel, scalars, arrays, outs, scratch=(), limit=8, specs=None):
    vmem = pl.BlockSpec(memory_space=pltpu.VMEM)
    smem = pl.BlockSpec(memory_space=pltpu.SMEM)
    return pl.pallas_call(
        kernel,
        out_shape=outs,
        in_specs=[smem] * len(scalars) + [vmem] * len(arrays),
        out_specs=specs or (vmem,) * len(outs),
        scratch_shapes=list(scratch),
        compiler_params=pltpu.CompilerParams(vmem_limit_bytes=limit * 2**20),
        cost_estimate=pl.CostEstimate(flops=1000, bytes_accessed=1000, transcendentals=0),
    )(*scalars, *arrays)


def shape(*size, dtype=jnp.bfloat16):
    return jax.ShapeDtypeStruct(size, dtype)


def spread_kernel(core_ref, w_ref, out_ref):
    f32 = jnp.float32
    lanes = pl.ds(pl.multiple_of(core_ref[0] * PART, PART), PART)
    sides = []
    for t in range(2):
        rows = []
        for core in range(NC):
            rows += [w_ref[core, r, :, lanes].astype(f32)[t : t + 1, :] for r in range(OWN)]
            rows.append(jnp.zeros((PAD - OWN, PART), f32))
        sides.append(jnp.concatenate(rows, axis=0))
    rows = jnp.concatenate(sides, axis=1).astype(out_ref.dtype)
    for copy in range(out_ref.shape[0]):
        out_ref[copy] = rows


def copies_kernel(block_ref, out_ref, sems):
    copies = [
        pltpu.make_async_copy(block_ref, out_ref.at[i], sems.at[i])
        for i in range(out_ref.shape[0])
    ]
    for copy in copies:
        copy.start()
    for copy in copies:
        copy.wait()


def pack_kernel(core_ref, q_ref, g_ref, near_ref, far_ref):
    for out_ref, side in ((near_ref, core_ref[0]), (far_ref, 1 - core_ref[0])):
        lanes = pl.ds(pl.multiple_of(side * PART, PART), PART)
        out_ref[:, :PART] = q_ref[:, lanes]
        out_ref[:, PART:] = g_ref[:, lanes]


def unpack_kernel(core_ref, mine_ref, got_ref, att_ref, qg_ref):
    core = core_ref[0]
    here = pl.ds(pl.multiple_of(core * PART, PART), PART)
    there = pl.ds(pl.multiple_of((1 - core) * PART, PART), PART)
    for out_ref, first in ((att_ref, 0), (qg_ref, PART)):
        out_ref[:, here] = mine_ref[:, first : first + PART]
        out_ref[:, there] = got_ref[:, first : first + PART]


def layout_kernel(own_ref, right_ref, left_ref, other_ref, x_ref):
    f32, b16 = jnp.float32, jnp.bfloat16
    place = lax.broadcasted_iota(jnp.int32, (1, ROWS), 1)
    pick = lax.broadcasted_iota(jnp.int32, (ENC, ROWS), 0) == natural_column(place)
    pick = jnp.where(pick, 1.0, 0.0).astype(b16)
    parts = [own_ref[...], right_ref[...], left_ref[...]]
    parts += [other_ref[i * NROWS : (i + 1) * NROWS, :] for i in range(3)]
    for i, part in enumerate(parts):
        x = jnp.dot(part, pick, preferred_element_type=f32)
        x_ref[i * NROWS : (i + 1) * NROWS, :] = x.astype(b16)


def attention_kernel(
    sel_ref, x_ref, w_ref, near_ref, far_ref,
    mine_ref, back_ref, cb_ref, share_ref, kv_ref, acc_ref, out_ref, sems,
):
    f32, b16 = jnp.float32, jnp.bfloat16
    factor = 1.0 / HD**0.5
    acc_ref[...] = jnp.zeros_like(acc_ref)
    kv_ref[...] = jnp.dot(x_ref[...], w_ref[...], preferred_element_type=f32).astype(b16)
    heads = PART // HD
    units = [(span, head) for span in range(4) for head in range(heads)]
    kcols = [slice(head * HD, (head + 1) * HD) for _, head in units]
    vcols = [slice(PART + head * HD, PART + (head + 1) * HD) for _, head in units]
    rows = [slice(span % 2 * SPAN, (span % 2 + 1) * SPAN) for span, _ in units]
    blocks = [
        [
            pl.ds(pl.multiple_of(sel_ref[span * NBR + j] * NROWS, NROWS), NROWS)
            for j in range(NBR)
        ]
        for span, _ in units
    ]
    q, g = [], []
    for (span, _), r, kc, vc in zip(units, rows, kcols, vcols):
        from_ref = near_ref if span < 2 else far_ref
        q.append(from_ref[r, kc])
        g.append(from_ref[r, vc])
    k = [jnp.concatenate([kv_ref[b, c] for b in two], axis=0) for two, c in zip(blocks, kcols)]
    v = [jnp.concatenate([kv_ref[b, c] for b in two], axis=0) for two, c in zip(blocks, vcols)]
    scores = [
        lax.dot_general(a, b, NT, preferred_element_type=f32) * factor for a, b in zip(q, k)
    ]
    dprobs = [lax.dot_general(a, b, NT, preferred_element_type=f32) for a, b in zip(g, v)]
    raised = [jnp.exp(a - jnp.max(a, axis=-1, keepdims=True)) for a in scores]
    probs = [a / jnp.sum(a, axis=-1, keepdims=True) for a in raised]
    probs_b = [a.astype(b16) for a in probs]
    delta = [jnp.sum(a * b, axis=-1, keepdims=True) for a, b in zip(probs, dprobs)]
    dscores = [
        (a * (b - c) * factor).astype(b16) for a, b, c in zip(probs, dprobs, delta)
    ]
    for i, (span, _) in enumerate(units):
        to_ref = mine_ref if span < 2 else back_ref
        out = jnp.dot(probs_b[i], v[i], preferred_element_type=f32)
        to_ref[rows[i], kcols[i]] = out.astype(b16)
        out = jnp.dot(dscores[i], k[i], preferred_element_type=f32)
        to_ref[rows[i], vcols[i]] = out.astype(b16)
    vgrad = [lax.dot_general(a, b, TN, preferred_element_type=f32) for a, b in zip(probs_b, g)]
    kgrad = [lax.dot_general(a, b, TN, preferred_element_type=f32) for a, b in zip(dscores, q)]
    for i in range(len(units)):
        for j, block in enumerate(blocks[i]):
            part = slice(j * NROWS, (j + 1) * NROWS)
            acc_ref[block, kcols[i]] += kgrad[i][part, :]
            acc_ref[block, vcols[i]] += vgrad[i][part, :]
    cb_ref[...] = acc_ref[...].astype(b16)
    copies = []
    for part in range(NY):
        size = out_ref.shape[1]
        rows = slice(part * size, (part + 1) * size)
        product = lax.dot_general(x_ref[:, rows], cb_ref[...], TN, preferred_element_type=f32)
        out_ref[part] = product.astype(b16)
        copies.append(pltpu.make_async_copy(out_ref.at[part], share_ref.at[part], sems.at[part]))
        copies[-1].start()
    for copy in copies:
        copy.wait()


def encoding_kernel(w_ref, cb_ref, keep_ref, send_ref):
    half = keep_ref.shape[0]
    for out_ref, first in ((keep_ref, 0), (send_ref, half)):
        out_ref[...] = lax.dot_general(
            cb_ref[first : first + half, :], w_ref[...], NT, preferred_element_type=jnp.float32
        ).astype(out_ref.dtype)


def merge_kernel(x_ref, keep_ref, got_ref, *out_refs):
    for step, out_ref in enumerate(out_refs):
        width = out_ref.shape[1]
        lanes = pl.ds(pl.multiple_of((x_ref[0] + step) % NX * width, width), width)
        total = keep_ref[:, lanes].astype(jnp.float32) + got_ref[:, lanes].astype(jnp.float32)
        out_ref[...] = total.astype(out_ref.dtype)


def summed(refs, rows):
    total = refs[0][rows, :].astype(jnp.float32)
    for ref in refs[1:]:
        total = total + ref[rows, :].astype(jnp.float32)
    return total


def groups_kernel(a_ref, b_ref, c_ref, d_ref, *out_refs):
    for slot, out_ref in enumerate(out_refs):
        rows = slice(slot * NROWS, (slot + 1) * NROWS)
        out_ref[...] = summed((a_ref, b_ref, c_ref, d_ref), rows).astype(out_ref.dtype)


def reduced_kernel(parts_ref, out_ref):
    total = parts_ref[0].astype(jnp.float32)
    for i in range(1, parts_ref.shape[0]):
        total = total + parts_ref[i].astype(jnp.float32)
    out_ref[...] = total.astype(out_ref.dtype)


def finish_kernel(own_ref, left_ref, right_ref, out_ref):
    b16 = jnp.bfloat16
    total = summed((own_ref, left_ref, right_ref), slice(None)).astype(b16)
    width, size = out_ref.shape[0], total.shape[1]
    column = natural_column(lax.broadcasted_iota(jnp.int32, (1, size), 1))
    pick = lax.broadcasted_iota(jnp.int32, (width, size), 0) == column
    pick = jnp.where(pick, 1.0, 0.0).astype(b16)
    out_ref[...] = lax.dot_general(
        pick, total, NT, preferred_element_type=jnp.float32
    ).astype(b16)


def per_device(queries, encodings, kv_weight, pair_list, cotangent):
    f32, b16 = jnp.float32, jnp.bfloat16
    core = lax.axis_index("c")
    core_id = core.reshape(1)
    chip = lax.axis_index("y") * NZ + lax.axis_index("z")
    hbm = pl.BlockSpec(memory_space=pltpu.HBM)
    vmem = pl.BlockSpec(memory_space=pltpu.VMEM)

    both = lax.all_gather(kv_weight, "c")
    (copies,) = small_call(spread_kernel, (core_id,), (both,), (shape(NZ, NC * PAD, SIDE),))
    w = lax.all_to_all(copies, "z", 0, 0).reshape(NZ * NC * PAD, SIDE)
    right = shifted(encodings, -2)
    left = shifted(encodings, 2)
    near, far = small_call(
        pack_kernel, (core_id,), (queries, cotangent), (shape(NROWS, SIDE),) * 2
    )
    far = swap_cores(far)
    pairs_far = swap_cores(pair_list)
    w = after(w, pairs_far)
    (copies,) = small_call(
        copies_kernel, (), (w,), (shape(NY, *w.shape),),
        [pltpu.SemaphoreType.DMA((NY,))], specs=(hbm,),
    )
    w = lax.all_to_all(copies, "y", 0, 0).reshape(ROWS, SIDE)
    here = after(encodings, copies)
    other = swap_cores(jnp.concatenate([here, right, left]))
    (x,) = small_call(
        layout_kernel, (), (encodings, right, left, other),
        (shape(NEAR * NROWS, ROWS),), limit=16,
    )

    pairs = jnp.concatenate([pair_list.reshape(-1), pairs_far.reshape(-1)])
    step = (pairs // NC - chip + NY * NZ) % (NY * NZ)
    place = jnp.where(step == 0, OWN_BLOCK, jnp.where(step == 1, RIGHT, LEFT))
    sel = (place + jnp.where(pairs % NC == core, 0, 3)).astype(jnp.int32)

    grads = shape(NEAR * NROWS, SIDE)
    chunk = shape(NY, ROWS // NY, SIDE)
    mine, back, contributions, share = small_call(
        attention_kernel, (sel,), (x, w, near, far),
        (shape(NROWS, SIDE), shape(NROWS, SIDE), grads, chunk),
        [
            pltpu.VMEM(grads.shape, b16),
            pltpu.VMEM(grads.shape, f32),
            pltpu.VMEM(chunk.shape, b16),
            pltpu.SemaphoreType.DMA((NY,)),
        ],
        limit=20, specs=(vmem, vmem, vmem, hbm),
    )
    parts = lax.all_to_all(share, "y", 0, 0)
    ekeep, esend = small_call(
        encoding_kernel, (), (w, after(contributions, share)), (shape(3 * NROWS, ROWS),) * 2,
        limit=16,
    )
    got = swap_cores(esend)
    x_id = lax.axis_index("x").reshape(1)
    groups = list(
        small_call(merge_kernel, (x_id,), (ekeep, got), (shape(3 * NROWS, ROWS // NX),) * NX)
    )
    for step in (1, 3, 2):
        groups[step] = lax.ppermute(
            groups[step], "x", [(i, (i + step) % NX) for i in range(NX)]
        )
    returned = swap_cores(back)
    parts = after(parts, groups[1], groups[3])
    (total,) = small_call(reduced_kernel, (), (parts,), (shape(ROWS // NY, SIDE),))
    parts = lax.all_to_all(total.reshape(NZ, NC * PAD, SIDE), "z", 0, 0)
    sums = lax.all_gather(jnp.sum(parts.astype(f32), axis=0), "c")
    sums = lax.dynamic_slice_in_dim(sums, core * PAD, OWN, 1).reshape(NC, OWN, 2, PART)
    weight_grad = sums.transpose(1, 2, 0, 3).reshape(OWN, 2, COLS // 2)

    groups[0] = after(groups[0], total)
    own, right, left = small_call(
        groups_kernel, (), groups, (shape(NROWS, ROWS // NX),) * 3
    )
    from_left = shifted(right, 2)
    from_right = shifted(left, -2)
    attended, query_grad = small_call(
        unpack_kernel, (core_id,), (mine, returned), (shape(NROWS, SIDE),) * 2
    )
    own = after(own, weight_grad)
    (flipped,) = small_call(
        finish_kernel, (), (own, from_left, from_right), (shape(ENC // NX, NROWS),)
    )
    return attended, query_grad, flipped.T, weight_grad


def solution(mesh):
    mesh = Mesh(mesh.devices.reshape(NY, NZ, NC, NX), ("y", "z", "c", "x"))
    return jax.shard_map(
        per_device,
        mesh=mesh,
        in_specs=(P(DP, "x"), P(DP, None), P(DP, None, "x"), P(DP, None), P(DP, "x")),
        out_specs=(P(DP, "x"), P(DP, "x"), P(DP, "x"), P(DP, None, "x")),
        check_vma=False,
    )
```

```python
import jax
import jax.numpy as jnp
from jax import lax
from jax.experimental import pallas as pl
from jax.experimental.pallas import tpu as pltpu
from jax.sharding import Mesh
from jax.sharding import PartitionSpec as P

HD = 128
SPAN = 64
NROWS = 128
NBR = 2
NY = 4
NZ = 16
NC = 2
NX = 4
DP = ("y", "z", "c")
ENC = 896
OWN = 7
PAD = 8
COLS = 1024
SIDE = COLS // NC
PART = COLS // (2 * NC)
ROWS = NY * NZ * NC * PAD
NEAR = 6
NT = (((1,), (1,)), ((), ()))
TN = (((0,), (0,)), ((), ()))
OWN_BLOCK, RIGHT, LEFT = range(3)


def after(value, *earlier):
    return lax.optimization_barrier((value,) + earlier)[0]


def swap_cores(value):
    return lax.ppermute(value, "c", [(0, 1), (1, 0)])


def shifted(value, steps):
    count = NY * NZ * NC
    return lax.ppermute(value, DP, [(i, (i + steps) % count) for i in range(count)])


def natural_column(place):
    row = place % PAD
    return jnp.where(row < OWN, place // PAD * OWN + row, -1)


def small_call(kernel, scalars, arrays, outs, scratch=(), limit=8, specs=None):
    vmem = pl.BlockSpec(memory_space=pltpu.VMEM)
    smem = pl.BlockSpec(memory_space=pltpu.SMEM)
    return pl.pallas_call(
        kernel,
        out_shape=outs,
        in_specs=[smem] * len(scalars) + [vmem] * len(arrays),
        out_specs=specs or (vmem,) * len(outs),
        scratch_shapes=list(scratch),
        compiler_params=pltpu.CompilerParams(vmem_limit_bytes=limit * 2**20),
        cost_estimate=pl.CostEstimate(flops=1000, bytes_accessed=1000, transcendentals=0),
    )(*scalars, *arrays)


def shape(*size, dtype=jnp.bfloat16):
    return jax.ShapeDtypeStruct(size, dtype)


def spread_kernel(core_ref, w_ref, out_ref):
    f32 = jnp.float32
    lanes = pl.ds(pl.multiple_of(core_ref[0] * PART, PART), PART)
    sides = []
    for t in range(2):
        rows = []
        for core in range(NC):
            rows += [w_ref[core, r, :, lanes].astype(f32)[t : t + 1, :] for r in range(OWN)]
            rows.append(jnp.zeros((PAD - OWN, PART), f32))
        sides.append(jnp.concatenate(rows, axis=0))
    rows = jnp.concatenate(sides, axis=1).astype(out_ref.dtype)
    for copy in range(out_ref.shape[0]):
        out_ref[copy] = rows


def copies_kernel(block_ref, out_ref, sems):
    copies = [
        pltpu.make_async_copy(block_ref, out_ref.at[i], sems.at[i])
        for i in range(out_ref.shape[0])
    ]
    for copy in copies:
        copy.start()
    for copy in copies:
        copy.wait()


def pack_kernel(core_ref, q_ref, g_ref, near_ref, far_ref):
    for out_ref, side in ((near_ref, core_ref[0]), (far_ref, 1 - core_ref[0])):
        lanes = pl.ds(pl.multiple_of(side * PART, PART), PART)
        out_ref[:, :PART] = q_ref[:, lanes]
        out_ref[:, PART:] = g_ref[:, lanes]


def unpack_kernel(core_ref, mine_ref, got_ref, att_ref, qg_ref):
    core = core_ref[0]
    here = pl.ds(pl.multiple_of(core * PART, PART), PART)
    there = pl.ds(pl.multiple_of((1 - core) * PART, PART), PART)
    for out_ref, first in ((att_ref, 0), (qg_ref, PART)):
        out_ref[:, here] = mine_ref[:, first : first + PART]
        out_ref[:, there] = got_ref[:, first : first + PART]


def layout_kernel(own_ref, right_ref, left_ref, other_ref, x_ref):
    f32, b16 = jnp.float32, jnp.bfloat16
    place = lax.broadcasted_iota(jnp.int32, (1, ROWS), 1)
    pick = lax.broadcasted_iota(jnp.int32, (ENC, ROWS), 0) == natural_column(place)
    pick = jnp.where(pick, 1.0, 0.0).astype(b16)
    parts = [own_ref[...], right_ref[...], left_ref[...]]
    parts += [other_ref[i * NROWS : (i + 1) * NROWS, :] for i in range(3)]
    for i, part in enumerate(parts):
        x = jnp.dot(part, pick, preferred_element_type=f32)
        x_ref[i * NROWS : (i + 1) * NROWS, :] = x.astype(b16)


def attention_kernel(
    sel_ref, x_ref, w_ref, near_ref, far_ref,
    mine_ref, back_ref, cb_ref, share_ref, kv_ref, acc_ref, out_ref, sems,
):
    f32, b16 = jnp.float32, jnp.bfloat16
    factor = 1.0 / HD**0.5
    acc_ref[...] = jnp.zeros_like(acc_ref)
    kv_ref[...] = jnp.dot(x_ref[...], w_ref[...], preferred_element_type=f32).astype(b16)
    heads = PART // HD
    units = [(span, head) for span in range(4) for head in range(heads)]
    kcols = [slice(head * HD, (head + 1) * HD) for _, head in units]
    vcols = [slice(PART + head * HD, PART + (head + 1) * HD) for _, head in units]
    rows = [slice(span % 2 * SPAN, (span % 2 + 1) * SPAN) for span, _ in units]
    blocks = [
        [
            pl.ds(pl.multiple_of(sel_ref[span * NBR + j] * NROWS, NROWS), NROWS)
            for j in range(NBR)
        ]
        for span, _ in units
    ]
    q, g = [], []
    for (span, _), r, kc, vc in zip(units, rows, kcols, vcols):
        from_ref = near_ref if span < 2 else far_ref
        q.append(from_ref[r, kc])
        g.append(from_ref[r, vc])
    k = [jnp.concatenate([kv_ref[b, c] for b in two], axis=0) for two, c in zip(blocks, kcols)]
    v = [jnp.concatenate([kv_ref[b, c] for b in two], axis=0) for two, c in zip(blocks, vcols)]
    scores = [
        lax.dot_general(a, b, NT, preferred_element_type=f32) * factor for a, b in zip(q, k)
    ]
    dprobs = [lax.dot_general(a, b, NT, preferred_element_type=f32) for a, b in zip(g, v)]
    raised = [jnp.exp(a - jnp.max(a, axis=-1, keepdims=True)) for a in scores]
    probs = [a / jnp.sum(a, axis=-1, keepdims=True) for a in raised]
    probs_b = [a.astype(b16) for a in probs]
    delta = [jnp.sum(a * b, axis=-1, keepdims=True) for a, b in zip(probs, dprobs)]
    dscores = [
        (a * (b - c) * factor).astype(b16) for a, b, c in zip(probs, dprobs, delta)
    ]
    for i, (span, _) in enumerate(units):
        to_ref = mine_ref if span < 2 else back_ref
        out = jnp.dot(probs_b[i], v[i], preferred_element_type=f32)
        to_ref[rows[i], kcols[i]] = out.astype(b16)
        out = jnp.dot(dscores[i], k[i], preferred_element_type=f32)
        to_ref[rows[i], vcols[i]] = out.astype(b16)
    vgrad = [lax.dot_general(a, b, TN, preferred_element_type=f32) for a, b in zip(probs_b, g)]
    kgrad = [lax.dot_general(a, b, TN, preferred_element_type=f32) for a, b in zip(dscores, q)]
    for i in range(len(units)):
        for j, block in enumerate(blocks[i]):
            part = slice(j * NROWS, (j + 1) * NROWS)
            acc_ref[block, kcols[i]] += kgrad[i][part, :]
            acc_ref[block, vcols[i]] += vgrad[i][part, :]
    cb_ref[...] = acc_ref[...].astype(b16)
    copies = []
    for part in range(NY):
        size = out_ref.shape[1]
        if part % 2 == 0:
            product = lax.dot_general(
                x_ref[:, part * size : (part + 2) * size], cb_ref[...], TN,
                preferred_element_type=f32,
            )
        first = part % 2 * size
        out_ref[part] = product[first : first + size, :].astype(b16)
        copies.append(pltpu.make_async_copy(out_ref.at[part], share_ref.at[part], sems.at[part]))
        copies[-1].start()
    for copy in copies:
        copy.wait()


def encoding_kernel(w_ref, cb_ref, keep_ref, send_ref):
    half = keep_ref.shape[0]
    part = lax.dot_general(cb_ref[...], w_ref[...], NT, preferred_element_type=jnp.float32)
    keep_ref[...] = part[:half, :].astype(keep_ref.dtype)
    send_ref[...] = part[half:, :].astype(send_ref.dtype)


def merge_kernel(x_ref, keep_ref, got_ref, *out_refs):
    for step, out_ref in enumerate(out_refs):
        width = out_ref.shape[1]
        lanes = pl.ds(pl.multiple_of((x_ref[0] + step) % NX * width, width), width)
        total = keep_ref[:, lanes].astype(jnp.float32) + got_ref[:, lanes].astype(jnp.float32)
        out_ref[...] = total.astype(out_ref.dtype)


def summed(refs, rows):
    total = refs[0][rows, :].astype(jnp.float32)
    for ref in refs[1:]:
        total = total + ref[rows, :].astype(jnp.float32)
    return total


def groups_kernel(a_ref, b_ref, c_ref, d_ref, *out_refs):
    for slot, out_ref in enumerate(out_refs):
        rows = slice(slot * NROWS, (slot + 1) * NROWS)
        out_ref[...] = summed((a_ref, b_ref, c_ref, d_ref), rows).astype(out_ref.dtype)


def reduced_kernel(parts_ref, out_ref):
    total = parts_ref[0].astype(jnp.float32)
    for i in range(1, parts_ref.shape[0]):
        total = total + parts_ref[i].astype(jnp.float32)
    out_ref[...] = total.astype(out_ref.dtype)


def finish_kernel(own_ref, left_ref, right_ref, out_ref):
    b16 = jnp.bfloat16
    total = summed((own_ref, left_ref, right_ref), slice(None)).astype(b16)
    width, size = out_ref.shape[0], total.shape[1]
    column = natural_column(lax.broadcasted_iota(jnp.int32, (1, size), 1))
    pick = lax.broadcasted_iota(jnp.int32, (width, size), 0) == column
    pick = jnp.where(pick, 1.0, 0.0).astype(b16)
    out_ref[...] = lax.dot_general(
        pick, total, NT, preferred_element_type=jnp.float32
    ).astype(b16)


def per_device(queries, encodings, kv_weight, pair_list, cotangent):
    f32, b16 = jnp.float32, jnp.bfloat16
    core = lax.axis_index("c")
    core_id = core.reshape(1)
    chip = lax.axis_index("y") * NZ + lax.axis_index("z")
    hbm = pl.BlockSpec(memory_space=pltpu.HBM)
    vmem = pl.BlockSpec(memory_space=pltpu.VMEM)

    both = lax.all_gather(kv_weight, "c")
    (copies,) = small_call(spread_kernel, (core_id,), (both,), (shape(NZ, NC * PAD, SIDE),))
    w = lax.all_to_all(copies, "z", 0, 0).reshape(NZ * NC * PAD, SIDE)
    right = shifted(encodings, -2)
    left = shifted(encodings, 2)
    near, far = small_call(
        pack_kernel, (core_id,), (queries, cotangent), (shape(NROWS, SIDE),) * 2
    )
    far = swap_cores(far)
    pairs_far = swap_cores(pair_list)
    w = after(w, pairs_far)
    (copies,) = small_call(
        copies_kernel, (), (w,), (shape(NY, *w.shape),),
        [pltpu.SemaphoreType.DMA((NY,))], specs=(hbm,),
    )
    w = lax.all_to_all(copies, "y", 0, 0).reshape(ROWS, SIDE)
    here = after(encodings, copies)
    other = swap_cores(jnp.concatenate([here, right, left]))
    (x,) = small_call(
        layout_kernel, (), (encodings, right, left, other),
        (shape(NEAR * NROWS, ROWS),), limit=16,
    )

    pairs = jnp.concatenate([pair_list.reshape(-1), pairs_far.reshape(-1)])
    step = (pairs // NC - chip + NY * NZ) % (NY * NZ)
    place = jnp.where(step == 0, OWN_BLOCK, jnp.where(step == 1, RIGHT, LEFT))
    sel = (place + jnp.where(pairs % NC == core, 0, 3)).astype(jnp.int32)

    grads = shape(NEAR * NROWS, SIDE)
    chunk = shape(NY, ROWS // NY, SIDE)
    mine, back, contributions, share = small_call(
        attention_kernel, (sel,), (x, w, near, far),
        (shape(NROWS, SIDE), shape(NROWS, SIDE), grads, chunk),
        [
            pltpu.VMEM(grads.shape, b16),
            pltpu.VMEM(grads.shape, f32),
            pltpu.VMEM(chunk.shape, b16),
            pltpu.SemaphoreType.DMA((NY,)),
        ],
        limit=20, specs=(vmem, vmem, vmem, hbm),
    )
    parts = lax.all_to_all(share, "y", 0, 0)
    ekeep, esend = small_call(
        encoding_kernel, (), (w, contributions),
        (shape(3 * NROWS, ROWS),) * 2,
        limit=16,
    )
    got = swap_cores(esend)
    x_id = lax.axis_index("x").reshape(1)
    groups = list(
        small_call(merge_kernel, (x_id,), (ekeep, got), (shape(3 * NROWS, ROWS // NX),) * NX)
    )
    for step in (1, 3, 2):
        groups[step] = lax.ppermute(
            groups[step], "x", [(i, (i + step) % NX) for i in range(NX)]
        )
    returned = swap_cores(back)
    parts = after(parts, groups[1], groups[3])
    (total,) = small_call(reduced_kernel, (), (parts,), (shape(ROWS // NY, SIDE),))
    parts = lax.all_to_all(total.reshape(NZ, NC * PAD, SIDE), "z", 0, 0)
    sums = lax.all_gather(jnp.sum(parts.astype(f32), axis=0), "c")
    sums = lax.dynamic_slice_in_dim(sums, core * PAD, OWN, 1).reshape(NC, OWN, 2, PART)
    weight_grad = sums.transpose(1, 2, 0, 3).reshape(OWN, 2, COLS // 2)

    groups[0] = after(groups[0], total)
    own, right, left = small_call(
        groups_kernel, (), groups, (shape(NROWS, ROWS // NX),) * 3
    )
    from_left = shifted(right, 2)
    from_right = shifted(left, -2)
    attended, query_grad = small_call(
        unpack_kernel, (core_id,), (mine, returned), (shape(NROWS, SIDE),) * 2
    )
    own = after(own, weight_grad)
    (flipped,) = small_call(
        finish_kernel, (), (own, from_left, from_right), (shape(ENC // NX, NROWS),)
    )
    return attended, query_grad, flipped.T, weight_grad


def solution(mesh):
    mesh = Mesh(mesh.devices.reshape(NY, NZ, NC, NX), ("y", "z", "c", "x"))
    return jax.shard_map(
        per_device,
        mesh=mesh,
        in_specs=(P(DP, "x"), P(DP, None), P(DP, None, "x"), P(DP, None), P(DP, "x")),
        out_specs=(P(DP, "x"), P(DP, "x"), P(DP, "x"), P(DP, None, "x")),
        check_vma=False,
    )
```

```python
import jax
import jax.numpy as jnp
from jax import lax
from jax.experimental import pallas as pl
from jax.experimental.pallas import tpu as pltpu
from jax.sharding import Mesh
from jax.sharding import PartitionSpec as P

HD = 128
SPAN = 64
NROWS = 128
NBR = 2
NY = 4
NZ = 16
NC = 2
NX = 4
DP = ("y", "z", "c")
ENC = 896
OWN = 7
PAD = 8
COLS = 1024
SIDE = COLS // NC
PART = COLS // (2 * NC)
ROWS = NY * NZ * NC * PAD
NEAR = 6
NT = (((1,), (1,)), ((), ()))
TN = (((0,), (0,)), ((), ()))
OWN_BLOCK, RIGHT, LEFT = range(3)


def after(value, *earlier):
    return lax.optimization_barrier((value,) + earlier)[0]


def swap_cores(value):
    return lax.ppermute(value, "c", [(0, 1), (1, 0)])


def shifted(value, steps):
    count = NY * NZ * NC
    return lax.ppermute(value, DP, [(i, (i + steps) % count) for i in range(count)])


def natural_column(place):
    row = place % PAD
    return jnp.where(row < OWN, place // PAD * OWN + row, -1)


def small_call(kernel, scalars, arrays, outs, scratch=(), limit=8, specs=None):
    vmem = pl.BlockSpec(memory_space=pltpu.VMEM)
    smem = pl.BlockSpec(memory_space=pltpu.SMEM)
    return pl.pallas_call(
        kernel,
        out_shape=outs,
        in_specs=[smem] * len(scalars) + [vmem] * len(arrays),
        out_specs=specs or (vmem,) * len(outs),
        scratch_shapes=list(scratch),
        compiler_params=pltpu.CompilerParams(vmem_limit_bytes=limit * 2**20),
        cost_estimate=pl.CostEstimate(flops=1000, bytes_accessed=1000, transcendentals=0),
    )(*scalars, *arrays)


def shape(*size, dtype=jnp.bfloat16):
    return jax.ShapeDtypeStruct(size, dtype)


def spread_kernel(core_ref, w_ref, out_ref):
    f32 = jnp.float32
    lanes = pl.ds(pl.multiple_of(core_ref[0] * PART, PART), PART)
    sides = []
    for t in range(2):
        rows = []
        for core in range(NC):
            rows += [w_ref[core, r, :, lanes].astype(f32)[t : t + 1, :] for r in range(OWN)]
            rows.append(jnp.zeros((PAD - OWN, PART), f32))
        sides.append(jnp.concatenate(rows, axis=0))
    rows = jnp.concatenate(sides, axis=1).astype(out_ref.dtype)
    for copy in range(out_ref.shape[0]):
        out_ref[copy] = rows


def copies_kernel(block_ref, out_ref, sems):
    copies = [
        pltpu.make_async_copy(block_ref, out_ref.at[i], sems.at[i])
        for i in range(out_ref.shape[0])
    ]
    for copy in copies:
        copy.start()
    for copy in copies:
        copy.wait()


def pack_kernel(core_ref, q_ref, g_ref, near_ref, far_ref):
    for out_ref, side in ((near_ref, core_ref[0]), (far_ref, 1 - core_ref[0])):
        lanes = pl.ds(pl.multiple_of(side * PART, PART), PART)
        out_ref[:, :PART] = q_ref[:, lanes]
        out_ref[:, PART:] = g_ref[:, lanes]


def unpack_kernel(core_ref, mine_ref, got_ref, att_ref, qg_ref):
    core = core_ref[0]
    here = pl.ds(pl.multiple_of(core * PART, PART), PART)
    there = pl.ds(pl.multiple_of((1 - core) * PART, PART), PART)
    for out_ref, first in ((att_ref, 0), (qg_ref, PART)):
        out_ref[:, here] = mine_ref[:, first : first + PART]
        out_ref[:, there] = got_ref[:, first : first + PART]


def layout_kernel(own_ref, right_ref, left_ref, other_ref, x_ref):
    f32, b16 = jnp.float32, jnp.bfloat16
    place = lax.broadcasted_iota(jnp.int32, (1, ROWS), 1)
    pick = lax.broadcasted_iota(jnp.int32, (ENC, ROWS), 0) == natural_column(place)
    pick = jnp.where(pick, 1.0, 0.0).astype(b16)
    parts = [own_ref[...], right_ref[...], left_ref[...]]
    parts += [other_ref[i * NROWS : (i + 1) * NROWS, :] for i in range(3)]
    for i, part in enumerate(parts):
        x = jnp.dot(part, pick, preferred_element_type=f32)
        x_ref[i * NROWS : (i + 1) * NROWS, :] = x.astype(b16)


def attention_kernel(
    sel_ref, x_ref, w_ref, near_ref, far_ref,
    mine_ref, back_ref, cb_ref, share_ref, kv_ref, acc_ref, out_ref, sems,
):
    f32, b16 = jnp.float32, jnp.bfloat16
    factor = 1.0 / HD**0.5
    acc_ref[...] = jnp.zeros_like(acc_ref)
    kv_ref[...] = jnp.dot(x_ref[...], w_ref[...], preferred_element_type=f32).astype(b16)
    heads = PART // HD
    units = [(span, head) for span in range(4) for head in range(heads)]
    kcols = [slice(head * HD, (head + 1) * HD) for _, head in units]
    vcols = [slice(PART + head * HD, PART + (head + 1) * HD) for _, head in units]
    rows = [slice(span % 2 * SPAN, (span % 2 + 1) * SPAN) for span, _ in units]
    blocks = [
        [
            pl.ds(pl.multiple_of(sel_ref[span * NBR + j] * NROWS, NROWS), NROWS)
            for j in range(NBR)
        ]
        for span, _ in units
    ]
    q, g = [], []
    for (span, _), r, kc, vc in zip(units, rows, kcols, vcols):
        from_ref = near_ref if span < 2 else far_ref
        q.append(from_ref[r, kc])
        g.append(from_ref[r, vc])
    k = [jnp.concatenate([kv_ref[b, c] for b in two], axis=0) for two, c in zip(blocks, kcols)]
    v = [jnp.concatenate([kv_ref[b, c] for b in two], axis=0) for two, c in zip(blocks, vcols)]
    scores = [
        lax.dot_general(a, b, NT, preferred_element_type=f32) * factor for a, b in zip(q, k)
    ]
    dprobs = [lax.dot_general(a, b, NT, preferred_element_type=f32) for a, b in zip(g, v)]
    raised = [jnp.exp(a - jnp.max(a, axis=-1, keepdims=True)) for a in scores]
    probs = [a / jnp.sum(a, axis=-1, keepdims=True) for a in raised]
    probs_b = [a.astype(b16) for a in probs]
    delta = [jnp.sum(a * b, axis=-1, keepdims=True) for a, b in zip(probs, dprobs)]
    dscores = [
        (a * (b - c) * factor).astype(b16) for a, b, c in zip(probs, dprobs, delta)
    ]
    vgrad = [lax.dot_general(a, b, TN, preferred_element_type=f32) for a, b in zip(probs_b, g)]
    kgrad = [lax.dot_general(a, b, TN, preferred_element_type=f32) for a, b in zip(dscores, q)]
    for i in range(len(units)):
        for j, block in enumerate(blocks[i]):
            part = slice(j * NROWS, (j + 1) * NROWS)
            acc_ref[block, kcols[i]] += kgrad[i][part, :]
            acc_ref[block, vcols[i]] += vgrad[i][part, :]
    cb_ref[...] = acc_ref[...].astype(b16)
    copies = []
    for part in range(NY):
        size = out_ref.shape[1]
        if part % 2 == 0:
            product = lax.dot_general(
                x_ref[:, part * size : (part + 2) * size], cb_ref[...], TN,
                preferred_element_type=f32,
            )
        first = part % 2 * size
        out_ref[part] = product[first : first + size, :].astype(b16)
        copies.append(pltpu.make_async_copy(out_ref.at[part], share_ref.at[part], sems.at[part]))
        copies[-1].start()
    for i, (span, _) in enumerate(units):
        to_ref = mine_ref if span < 2 else back_ref
        out = jnp.dot(probs_b[i], v[i], preferred_element_type=f32)
        to_ref[rows[i], kcols[i]] = out.astype(b16)
        out = jnp.dot(dscores[i], k[i], preferred_element_type=f32)
        to_ref[rows[i], vcols[i]] = out.astype(b16)
    for copy in copies:
        copy.wait()


def encoding_kernel(w_ref, cb_ref, keep_ref, send_ref):
    half = keep_ref.shape[0]
    part = lax.dot_general(cb_ref[...], w_ref[...], NT, preferred_element_type=jnp.float32)
    keep_ref[...] = part[:half, :].astype(keep_ref.dtype)
    send_ref[...] = part[half:, :].astype(send_ref.dtype)


def merge_kernel(x_ref, keep_ref, got_ref, *out_refs):
    for step, out_ref in enumerate(out_refs):
        width = out_ref.shape[1]
        lanes = pl.ds(pl.multiple_of((x_ref[0] + step) % NX * width, width), width)
        total = keep_ref[:, lanes].astype(jnp.float32) + got_ref[:, lanes].astype(jnp.float32)
        out_ref[...] = total.astype(out_ref.dtype)


def summed(refs, rows):
    total = refs[0][rows, :].astype(jnp.float32)
    for ref in refs[1:]:
        total = total + ref[rows, :].astype(jnp.float32)
    return total


def groups_kernel(a_ref, b_ref, c_ref, d_ref, *out_refs):
    for slot, out_ref in enumerate(out_refs):
        rows = slice(slot * NROWS, (slot + 1) * NROWS)
        out_ref[...] = summed((a_ref, b_ref, c_ref, d_ref), rows).astype(out_ref.dtype)


def reduced_kernel(parts_ref, out_ref):
    total = parts_ref[0].astype(jnp.float32)
    for i in range(1, parts_ref.shape[0]):
        total = total + parts_ref[i].astype(jnp.float32)
    out_ref[...] = total.astype(out_ref.dtype)


def finish_kernel(own_ref, left_ref, right_ref, out_ref):
    b16 = jnp.bfloat16
    total = summed((own_ref, left_ref, right_ref), slice(None)).astype(b16)
    width, size = out_ref.shape[0], total.shape[1]
    column = natural_column(lax.broadcasted_iota(jnp.int32, (1, size), 1))
    pick = lax.broadcasted_iota(jnp.int32, (width, size), 0) == column
    pick = jnp.where(pick, 1.0, 0.0).astype(b16)
    out_ref[...] = lax.dot_general(
        pick, total, NT, preferred_element_type=jnp.float32
    ).astype(b16)


def per_device(queries, encodings, kv_weight, pair_list, cotangent):
    f32, b16 = jnp.float32, jnp.bfloat16
    core = lax.axis_index("c")
    core_id = core.reshape(1)
    chip = lax.axis_index("y") * NZ + lax.axis_index("z")
    hbm = pl.BlockSpec(memory_space=pltpu.HBM)
    vmem = pl.BlockSpec(memory_space=pltpu.VMEM)

    both = lax.all_gather(kv_weight, "c")
    (copies,) = small_call(spread_kernel, (core_id,), (both,), (shape(NZ, NC * PAD, SIDE),))
    w = lax.all_to_all(copies, "z", 0, 0).reshape(NZ * NC * PAD, SIDE)
    right = shifted(encodings, -2)
    left = shifted(encodings, 2)
    near, far = small_call(
        pack_kernel, (core_id,), (queries, cotangent), (shape(NROWS, SIDE),) * 2
    )
    far = swap_cores(far)
    pairs_far = swap_cores(pair_list)
    w = after(w, pairs_far)
    (copies,) = small_call(
        copies_kernel, (), (w,), (shape(NY, *w.shape),),
        [pltpu.SemaphoreType.DMA((NY,))], specs=(hbm,),
    )
    w = lax.all_to_all(copies, "y", 0, 0).reshape(ROWS, SIDE)
    here = after(encodings, copies)
    other = swap_cores(jnp.concatenate([here, right, left]))
    (x,) = small_call(
        layout_kernel, (), (encodings, right, left, other),
        (shape(NEAR * NROWS, ROWS),), limit=16,
    )

    pairs = jnp.concatenate([pair_list.reshape(-1), pairs_far.reshape(-1)])
    step = (pairs // NC - chip + NY * NZ) % (NY * NZ)
    place = jnp.where(step == 0, OWN_BLOCK, jnp.where(step == 1, RIGHT, LEFT))
    sel = (place + jnp.where(pairs % NC == core, 0, 3)).astype(jnp.int32)

    grads = shape(NEAR * NROWS, SIDE)
    chunk = shape(NY, ROWS // NY, SIDE)
    mine, back, contributions, share = small_call(
        attention_kernel, (sel,), (x, w, near, far),
        (shape(NROWS, SIDE), shape(NROWS, SIDE), grads, chunk),
        [
            pltpu.VMEM(grads.shape, b16),
            pltpu.VMEM(grads.shape, f32),
            pltpu.VMEM(chunk.shape, b16),
            pltpu.SemaphoreType.DMA((NY,)),
        ],
        limit=20, specs=(vmem, vmem, vmem, hbm),
    )
    parts = lax.all_to_all(share, "y", 0, 0)
    ekeep, esend = small_call(
        encoding_kernel, (), (w, contributions),
        (shape(3 * NROWS, ROWS),) * 2,
        limit=16,
    )
    got = swap_cores(esend)
    x_id = lax.axis_index("x").reshape(1)
    groups = list(
        small_call(merge_kernel, (x_id,), (ekeep, got), (shape(3 * NROWS, ROWS // NX),) * NX)
    )
    for step in (1, 3, 2):
        groups[step] = lax.ppermute(
            groups[step], "x", [(i, (i + step) % NX) for i in range(NX)]
        )
    returned = swap_cores(back)
    parts = after(parts, groups[1], groups[3])
    (total,) = small_call(reduced_kernel, (), (parts,), (shape(ROWS // NY, SIDE),))
    parts = lax.all_to_all(total.reshape(NZ, NC * PAD, SIDE), "z", 0, 0)
    sums = lax.all_gather(jnp.sum(parts.astype(f32), axis=0), "c")
    sums = lax.dynamic_slice_in_dim(sums, core * PAD, OWN, 1).reshape(NC, OWN, 2, PART)
    weight_grad = sums.transpose(1, 2, 0, 3).reshape(OWN, 2, COLS // 2)

    groups[0] = after(groups[0], total)
    own, right, left = small_call(
        groups_kernel, (), groups, (shape(NROWS, ROWS // NX),) * 3
    )
    from_left = shifted(right, 2)
    from_right = shifted(left, -2)
    attended, query_grad = small_call(
        unpack_kernel, (core_id,), (mine, returned), (shape(NROWS, SIDE),) * 2
    )
    own = after(own, weight_grad)
    (flipped,) = small_call(
        finish_kernel, (), (own, from_left, from_right), (shape(ENC // NX, NROWS),)
    )
    return attended, query_grad, flipped.T, weight_grad


def solution(mesh):
    mesh = Mesh(mesh.devices.reshape(NY, NZ, NC, NX), ("y", "z", "c", "x"))
    return jax.shard_map(
        per_device,
        mesh=mesh,
        in_specs=(P(DP, "x"), P(DP, None), P(DP, None, "x"), P(DP, None), P(DP, "x")),
        out_specs=(P(DP, "x"), P(DP, "x"), P(DP, "x"), P(DP, None, "x")),
        check_vma=False,
    )
```

```python
import jax
import jax.numpy as jnp
from jax import lax
from jax.experimental import pallas as pl
from jax.experimental.pallas import tpu as pltpu
from jax.sharding import Mesh
from jax.sharding import PartitionSpec as P

HD = 128
SPAN = 64
NROWS = 128
NBR = 2
NY = 4
NZ = 16
NC = 2
NX = 4
DP = ("y", "z", "c")
ENC = 896
OWN = 7
PAD = 8
COLS = 1024
SIDE = COLS // NC
PART = COLS // (2 * NC)
ROWS = NY * NZ * NC * PAD
NEAR = 6
NT = (((1,), (1,)), ((), ()))
TN = (((0,), (0,)), ((), ()))
OWN_BLOCK, RIGHT, LEFT = range(3)


def after(value, *earlier):
    return lax.optimization_barrier((value,) + earlier)[0]


def swap_cores(value):
    return lax.ppermute(value, "c", [(0, 1), (1, 0)])


def shifted(value, steps):
    count = NY * NZ * NC
    return lax.ppermute(value, DP, [(i, (i + steps) % count) for i in range(count)])


def natural_column(place):
    row = place % PAD
    return jnp.where(row < OWN, place // PAD * OWN + row, -1)


def small_call(kernel, scalars, arrays, outs, scratch=(), limit=8, specs=None):
    vmem = pl.BlockSpec(memory_space=pltpu.VMEM)
    smem = pl.BlockSpec(memory_space=pltpu.SMEM)
    return pl.pallas_call(
        kernel,
        out_shape=outs,
        in_specs=[smem] * len(scalars) + [vmem] * len(arrays),
        out_specs=specs or (vmem,) * len(outs),
        scratch_shapes=list(scratch),
        compiler_params=pltpu.CompilerParams(vmem_limit_bytes=limit * 2**20),
        cost_estimate=pl.CostEstimate(flops=1000, bytes_accessed=1000, transcendentals=0),
    )(*scalars, *arrays)


def shape(*size, dtype=jnp.bfloat16):
    return jax.ShapeDtypeStruct(size, dtype)


def spread_kernel(core_ref, w_ref, out_ref):
    f32 = jnp.float32
    lanes = pl.ds(pl.multiple_of(core_ref[0] * PART, PART), PART)
    sides = []
    for t in range(2):
        rows = []
        for core in range(NC):
            rows += [w_ref[core, r, :, lanes].astype(f32)[t : t + 1, :] for r in range(OWN)]
            rows.append(jnp.zeros((PAD - OWN, PART), f32))
        sides.append(jnp.concatenate(rows, axis=0))
    rows = jnp.concatenate(sides, axis=1).astype(out_ref.dtype)
    for copy in range(out_ref.shape[0]):
        out_ref[copy] = rows


def copies_kernel(block_ref, out_ref, sems):
    copies = [
        pltpu.make_async_copy(block_ref, out_ref.at[i], sems.at[i])
        for i in range(out_ref.shape[0])
    ]
    for copy in copies:
        copy.start()
    for copy in copies:
        copy.wait()


def pack_kernel(core_ref, q_ref, g_ref, near_ref, far_ref):
    for out_ref, side in ((near_ref, core_ref[0]), (far_ref, 1 - core_ref[0])):
        lanes = pl.ds(pl.multiple_of(side * PART, PART), PART)
        out_ref[:, :PART] = q_ref[:, lanes]
        out_ref[:, PART:] = g_ref[:, lanes]


def unpack_kernel(core_ref, mine_ref, got_ref, att_ref, qg_ref):
    core = core_ref[0]
    here = pl.ds(pl.multiple_of(core * PART, PART), PART)
    there = pl.ds(pl.multiple_of((1 - core) * PART, PART), PART)
    for out_ref, first in ((att_ref, 0), (qg_ref, PART)):
        out_ref[:, here] = mine_ref[:, first : first + PART]
        out_ref[:, there] = got_ref[:, first : first + PART]


def layout_kernel(own_ref, right_ref, left_ref, other_ref, x_ref):
    f32, b16 = jnp.float32, jnp.bfloat16
    place = lax.broadcasted_iota(jnp.int32, (1, ROWS), 1)
    pick = lax.broadcasted_iota(jnp.int32, (ENC, ROWS), 0) == natural_column(place)
    pick = jnp.where(pick, 1.0, 0.0).astype(b16)
    parts = [own_ref[...], right_ref[...], left_ref[...]]
    parts += [other_ref[i * NROWS : (i + 1) * NROWS, :] for i in range(3)]
    for i, part in enumerate(parts):
        x = jnp.dot(part, pick, preferred_element_type=f32)
        x_ref[i * NROWS : (i + 1) * NROWS, :] = x.astype(b16)


def attention_kernel(
    sel_ref, x_ref, w_ref, near_ref, far_ref,
    mine_ref, back_ref, cb_ref, share_ref, kv_ref, acc_ref, out_ref, sems,
):
    f32, b16 = jnp.float32, jnp.bfloat16
    factor = 1.0 / HD**0.5
    acc_ref[...] = jnp.zeros_like(acc_ref)
    kv_ref[...] = jnp.dot(x_ref[...], w_ref[...], preferred_element_type=f32).astype(b16)
    heads = PART // HD
    units = [(span, head) for span in range(4) for head in range(heads)]
    kcols = [slice(head * HD, (head + 1) * HD) for _, head in units]
    vcols = [slice(PART + head * HD, PART + (head + 1) * HD) for _, head in units]
    rows = [slice(span % 2 * SPAN, (span % 2 + 1) * SPAN) for span, _ in units]
    blocks = [
        [
            pl.ds(pl.multiple_of(sel_ref[span * NBR + j] * NROWS, NROWS), NROWS)
            for j in range(NBR)
        ]
        for span, _ in units
    ]
    q, g = [], []
    for (span, _), r, kc, vc in zip(units, rows, kcols, vcols):
        from_ref = near_ref if span < 2 else far_ref
        q.append(from_ref[r, kc])
        g.append(from_ref[r, vc])
    k = [jnp.concatenate([kv_ref[b, c] for b in two], axis=0) for two, c in zip(blocks, kcols)]
    v = [jnp.concatenate([kv_ref[b, c] for b in two], axis=0) for two, c in zip(blocks, vcols)]
    scores = [
        lax.dot_general(a, b, NT, preferred_element_type=f32) * factor for a, b in zip(q, k)
    ]
    dprobs = [lax.dot_general(a, b, NT, preferred_element_type=f32) for a, b in zip(g, v)]
    raised = [jnp.exp(a - jnp.max(a, axis=-1, keepdims=True)) for a in scores]
    probs = [a / jnp.sum(a, axis=-1, keepdims=True) for a in raised]
    probs_b = [a.astype(b16) for a in probs]
    delta = [jnp.sum(a * b, axis=-1, keepdims=True) for a, b in zip(probs, dprobs)]
    dscores = [
        (a * (b - c) * factor).astype(b16) for a, b, c in zip(probs, dprobs, delta)
    ]
    for i, (span, _) in enumerate(units):
        to_ref = mine_ref if span < 2 else back_ref
        out = jnp.dot(probs_b[i], v[i], preferred_element_type=f32)
        to_ref[rows[i], kcols[i]] = out.astype(b16)
        out = jnp.dot(dscores[i], k[i], preferred_element_type=f32)
        to_ref[rows[i], vcols[i]] = out.astype(b16)
    vgrad = [lax.dot_general(a, b, TN, preferred_element_type=f32) for a, b in zip(probs_b, g)]
    kgrad = [lax.dot_general(a, b, TN, preferred_element_type=f32) for a, b in zip(dscores, q)]
    for i in range(len(units)):
        for j, block in enumerate(blocks[i]):
            part = slice(j * NROWS, (j + 1) * NROWS)
            acc_ref[block, kcols[i]] += kgrad[i][part, :]
            acc_ref[block, vcols[i]] += vgrad[i][part, :]
    cb_ref[...] = acc_ref[...].astype(b16)
    copies = []
    product = lax.dot_general(x_ref[...], cb_ref[...], TN, preferred_element_type=f32)
    for part in range(NY):
        size = out_ref.shape[1]
        out_ref[part] = product[part * size : (part + 1) * size, :].astype(b16)
        copies.append(pltpu.make_async_copy(out_ref.at[part], share_ref.at[part], sems.at[part]))
        copies[-1].start()
    for copy in copies:
        copy.wait()


def encoding_kernel(w_ref, cb_ref, keep_ref, send_ref):
    half = keep_ref.shape[0]
    part = lax.dot_general(cb_ref[...], w_ref[...], NT, preferred_element_type=jnp.float32)
    keep_ref[...] = part[:half, :].astype(keep_ref.dtype)
    send_ref[...] = part[half:, :].astype(send_ref.dtype)


def merge_kernel(x_ref, keep_ref, got_ref, *out_refs):
    for step, out_ref in enumerate(out_refs):
        width = out_ref.shape[1]
        lanes = pl.ds(pl.multiple_of((x_ref[0] + step) % NX * width, width), width)
        total = keep_ref[:, lanes].astype(jnp.float32) + got_ref[:, lanes].astype(jnp.float32)
        out_ref[...] = total.astype(out_ref.dtype)


def summed(refs, rows):
    total = refs[0][rows, :].astype(jnp.float32)
    for ref in refs[1:]:
        total = total + ref[rows, :].astype(jnp.float32)
    return total


def groups_kernel(a_ref, b_ref, c_ref, d_ref, *out_refs):
    for slot, out_ref in enumerate(out_refs):
        rows = slice(slot * NROWS, (slot + 1) * NROWS)
        out_ref[...] = summed((a_ref, b_ref, c_ref, d_ref), rows).astype(out_ref.dtype)


def reduced_kernel(parts_ref, out_ref):
    total = parts_ref[0].astype(jnp.float32)
    for i in range(1, parts_ref.shape[0]):
        total = total + parts_ref[i].astype(jnp.float32)
    out_ref[...] = total.astype(out_ref.dtype)


def finish_kernel(own_ref, left_ref, right_ref, out_ref):
    b16 = jnp.bfloat16
    total = summed((own_ref, left_ref, right_ref), slice(None)).astype(b16)
    width, size = out_ref.shape[0], total.shape[1]
    column = natural_column(lax.broadcasted_iota(jnp.int32, (1, size), 1))
    pick = lax.broadcasted_iota(jnp.int32, (width, size), 0) == column
    pick = jnp.where(pick, 1.0, 0.0).astype(b16)
    out_ref[...] = lax.dot_general(
        pick, total, NT, preferred_element_type=jnp.float32
    ).astype(b16)


def per_device(queries, encodings, kv_weight, pair_list, cotangent):
    f32, b16 = jnp.float32, jnp.bfloat16
    core = lax.axis_index("c")
    core_id = core.reshape(1)
    chip = lax.axis_index("y") * NZ + lax.axis_index("z")
    hbm = pl.BlockSpec(memory_space=pltpu.HBM)
    vmem = pl.BlockSpec(memory_space=pltpu.VMEM)

    both = lax.all_gather(kv_weight, "c")
    (copies,) = small_call(spread_kernel, (core_id,), (both,), (shape(NZ, NC * PAD, SIDE),))
    w = lax.all_to_all(copies, "z", 0, 0).reshape(NZ * NC * PAD, SIDE)
    right = shifted(encodings, -2)
    left = shifted(encodings, 2)
    near, far = small_call(
        pack_kernel, (core_id,), (queries, cotangent), (shape(NROWS, SIDE),) * 2
    )
    far = swap_cores(far)
    pairs_far = swap_cores(pair_list)
    w = after(w, pairs_far)
    (copies,) = small_call(
        copies_kernel, (), (w,), (shape(NY, *w.shape),),
        [pltpu.SemaphoreType.DMA((NY,))], specs=(hbm,),
    )
    w = lax.all_to_all(copies, "y", 0, 0).reshape(ROWS, SIDE)
    here = after(encodings, copies)
    other = swap_cores(jnp.concatenate([here, right, left]))
    (x,) = small_call(
        layout_kernel, (), (encodings, right, left, other),
        (shape(NEAR * NROWS, ROWS),), limit=16,
    )

    pairs = jnp.concatenate([pair_list.reshape(-1), pairs_far.reshape(-1)])
    step = (pairs // NC - chip + NY * NZ) % (NY * NZ)
    place = jnp.where(step == 0, OWN_BLOCK, jnp.where(step == 1, RIGHT, LEFT))
    sel = (place + jnp.where(pairs % NC == core, 0, 3)).astype(jnp.int32)

    grads = shape(NEAR * NROWS, SIDE)
    chunk = shape(NY, ROWS // NY, SIDE)
    mine, back, contributions, share = small_call(
        attention_kernel, (sel,), (x, w, near, far),
        (shape(NROWS, SIDE), shape(NROWS, SIDE), grads, chunk),
        [
            pltpu.VMEM(grads.shape, b16),
            pltpu.VMEM(grads.shape, f32),
            pltpu.VMEM(chunk.shape, b16),
            pltpu.SemaphoreType.DMA((NY,)),
        ],
        limit=20, specs=(vmem, vmem, vmem, hbm),
    )
    parts = lax.all_to_all(share, "y", 0, 0)
    ekeep, esend = small_call(
        encoding_kernel, (), (w, contributions),
        (shape(3 * NROWS, ROWS),) * 2,
        limit=16,
    )
    got = swap_cores(esend)
    x_id = lax.axis_index("x").reshape(1)
    groups = list(
        small_call(merge_kernel, (x_id,), (ekeep, got), (shape(3 * NROWS, ROWS // NX),) * NX)
    )
    for step in (1, 3, 2):
        groups[step] = lax.ppermute(
            groups[step], "x", [(i, (i + step) % NX) for i in range(NX)]
        )
    returned = swap_cores(back)
    parts = after(parts, groups[1], groups[3])
    (total,) = small_call(reduced_kernel, (), (parts,), (shape(ROWS // NY, SIDE),))
    parts = lax.all_to_all(total.reshape(NZ, NC * PAD, SIDE), "z", 0, 0)
    sums = lax.all_gather(jnp.sum(parts.astype(f32), axis=0), "c")
    sums = lax.dynamic_slice_in_dim(sums, core * PAD, OWN, 1).reshape(NC, OWN, 2, PART)
    weight_grad = sums.transpose(1, 2, 0, 3).reshape(OWN, 2, COLS // 2)

    groups[0] = after(groups[0], total)
    own, right, left = small_call(
        groups_kernel, (), groups, (shape(NROWS, ROWS // NX),) * 3
    )
    from_left = shifted(right, 2)
    from_right = shifted(left, -2)
    attended, query_grad = small_call(
        unpack_kernel, (core_id,), (mine, returned), (shape(NROWS, SIDE),) * 2
    )
    own = after(own, weight_grad)
    (flipped,) = small_call(
        finish_kernel, (), (own, from_left, from_right), (shape(ENC // NX, NROWS),)
    )
    return attended, query_grad, flipped.T, weight_grad


def solution(mesh):
    mesh = Mesh(mesh.devices.reshape(NY, NZ, NC, NX), ("y", "z", "c", "x"))
    return jax.shard_map(
        per_device,
        mesh=mesh,
        in_specs=(P(DP, "x"), P(DP, None), P(DP, None, "x"), P(DP, None), P(DP, "x")),
        out_specs=(P(DP, "x"), P(DP, "x"), P(DP, "x"), P(DP, None, "x")),
        check_vma=False,
    )
```
